128 devices in a mesh: dp: 4 (over x_lo, core), expert: 32 (over z, y, x_hi).
Axes of the slice: x: 4 (x_hi: 2, x_lo: 2; x = x_hi * 2 + x_lo), y: 4, z: 4, core: 2. Of those that a mesh axis runs over, the one named last changes fastest.
Arguments:
- tokens: bfloat16 [16384, 5120], P(('dp', 'expert')), may hold values from -6 to 6
- router: bfloat16 [5120, 160], replicated, may hold values from -0.078125 to 0.078125
- expert_ids: int32 [16384, 6], P(('dp', 'expert')), may hold values from 0 to 31, all different within a row
- w_up: bfloat16 [32, 5120, 768], P('expert'), may hold values from -0.078125 to 0.078125
- w_down: bfloat16 [32, 768, 5120], P('expert'), may hold values from -0.21650635 to 0.21650635
- readout: bfloat16 [16384, 5120], P(('dp', 'expert')), may hold values from -0.078125 to 0.078125
- ref_logp: float32 [16384], P(('dp', 'expert')), may hold values from -3 to 3
- labels: int32 [128], P(('dp', 'expert')), may hold values 0 or 1
- prompt_read: bfloat16 [128, 5120], P(('dp', 'expert')), may hold values from -0.0074115883 to 0.0074115883
- kl_pair: int32 [128], P(('dp', 'expert')), may hold values from 0 to 31, as said below
- kl_ref: float32 [128], P(('dp', 'expert')), may hold values from 0 to 72
Outputs:
- grad_up: bfloat16 [32, 5120, 768], P('expert', 'dp')
- grad_down: bfloat16 [32, 768, 5120], P('expert', None, 'dp')
- losses: float32 [128], P(('dp', 'expert'))
- kl_terms: float32 [128], P(('dp', 'expert'))
The draws below stay inside these ranges and needn't reach their ends.
Inputs may be any that keep to these rules, and one draw needn't show every extreme that they name: `expert_ids`: each row names 6 different experts. `kl_pair`: the position, among the 32 examples of the example's own data-parallel group, of another example of that group; never the example's own position.
All inputs are finite; a program needn't handle non-finite values. No bound on the sum of `labels` on one device may be relied on, other than what follows from the above.
Results may differ from the reference program's by a relative error of at most 0.015.
Values may be sent and summed in bfloat16 or wider, within the bound.
A program may use at most 192 MiB of HBM per device.

```python
import jax
import jax.numpy as jnp
from jax import lax

D = 5120
E_ALL = 160
FH = 768
TOPK = 6
SEQ = 128
TOK_DEV = 128
EXPERTS = 32
CAP = 19
TOKENS = 16384
EXAMPLES = 128
GROUP_EX = 32
N_DP = 4
N_EXPERT = 32


def common_signs(key, columns):
    return jnp.where(jax.random.bernoulli(key, 0.5, (columns,)), 1.0, -1.0).astype(jnp.float32)


def draw_tokens(key, part):
    signs = common_signs(key, D)
    key = jax.random.fold_in(key, 31)
    noise = jnp.clip(jax.random.normal(key, (TOKENS, D), jnp.float32), -5.5, 5.5)
    return (noise + 0.1 * signs[None, :]).astype(jnp.bfloat16)


def draw_w_down(key, part):
    signs = common_signs(key, D)
    key = jax.random.fold_in(key, 37)
    spread = 1.0 / FH ** 0.5
    noise = jnp.clip(jax.random.normal(key, (EXPERTS, FH, D), jnp.float32), -5.0, 5.0)
    return (spread * noise + 1.5 / FH * signs[None, None, :]).astype(jnp.bfloat16)


def draw_prompt_read(key, part):
    signs = common_signs(key, D)
    key = jax.random.fold_in(key, 41)
    spread = 1.0 / (D * SEQ) ** 0.5
    noise = jnp.clip(jax.random.normal(key, (EXAMPLES, D), jnp.float32), -5.0, 5.0)
    return (spread * (noise + 0.05 * signs[None, :])).astype(jnp.bfloat16)


def draw_kl_pair(key, part):
    key = jax.random.fold_in(key, 11)
    own_place = jnp.arange(EXAMPLES, dtype=jnp.int32) % GROUP_EX
    offset = jax.random.randint(key, (EXAMPLES,), 1, GROUP_EX, dtype=jnp.int32)
    return (own_place + offset) % GROUP_EX


def draw_kl_ref(key, part):
    key = jax.random.fold_in(key, 23)
    position = jnp.arange(EXAMPLES, dtype=jnp.float32) / EXAMPLES
    baseline = jax.random.uniform(key, (EXAMPLES,), jnp.float32, 0.0, 8.0)
    return (1.0 + 2.0 * position) * baseline


def plant(entries, key, low, largest):
    longest = entries.shape.index(max(entries.shape))
    spots = []
    for shift in (0, 1):
        where = [jax.random.randint(jax.random.fold_in(key, axis), (), 0, length) for axis, length in enumerate(entries.shape)]
        where[longest] = (where[longest] + shift) % entries.shape[longest]
        spots.append(tuple(where))
    return entries.at[spots[0]].set(low).at[spots[1]].set(largest)


def block_scale(stream_key, shape, cuts, low, top_value):
    def one(dim, shards_of):
        draws = jax.random.uniform(jax.random.fold_in(jax.random.fold_in(stream_key, 6), dim), (shards_of,), jnp.float32, low / len(cuts), top_value / len(cuts))
        return jnp.repeat(jnp.exp(draws), shape[dim] // shards_of).reshape((-1,) + (1,) * (len(shape) - dim - 1))

    gain = one(*cuts[0])
    for cut in cuts[1:]:
        gain = gain * one(*cut)
    return gain


def different_ones(stream_key, rows, count, top, lift):
    order = jax.random.permutation(jax.random.fold_in(stream_key, 1), count)
    favour = order
    for power in range(3):
        favour = favour * favour // count
    favour = favour * lift // count
    chance = jax.random.randint(jax.random.fold_in(stream_key, 2), (rows, count), 0, 4096) + favour
    fixed_rows = jax.random.permutation(jax.random.fold_in(stream_key, 3), rows)[jnp.arange(count) % rows]
    chance = jnp.where(jnp.arange(rows)[:, None] == fixed_rows[None, :], 1 << 14, chance)
    priority = chance * count + jnp.arange(count)
    return lax.top_k(priority.astype(jnp.int32), top)[1].astype(jnp.int32)


def normal_values(stream_key, dims, deviation, limit, cuts=(), kind=jnp.bfloat16):
    array = deviation * jax.random.normal(stream_key, dims, jnp.float32)
    if cuts:
        array = array * block_scale(stream_key, dims, cuts, -0.22, 0.18)
    return jnp.clip(array, -limit, limit).astype(kind)


def setup_inputs(seed: int = 0) -> dict:
    key_of = jax.random.split(jax.random.key(seed), 12)
    return {
        "tokens": draw_tokens(jax.random.fold_in(key_of[11], 71), 0),
        "router": normal_values(key_of[1], (D, E_ALL), D ** -0.5, 0.078125),
        "expert_ids": different_ones(key_of[2], TOKENS, EXPERTS, TOPK, 1536),
        "w_up": normal_values(key_of[3], (EXPERTS, D, FH), D ** -0.5, 0.078125, ((0, 32),)),
        "w_down": draw_w_down(jax.random.fold_in(key_of[11], 71), 0),
        "readout": normal_values(key_of[5], (TOKENS, D), D ** -0.5, 0.078125, ((0, 128),)),
        "ref_logp": normal_values(key_of[6], (TOKENS,), 0.5, 3.0, ((0, 128),), jnp.float32),
        "labels": plant((jax.random.randint(key_of[7], (EXAMPLES,), 0, 2) < 1).astype(jnp.int32), jax.random.fold_in(key_of[7], 1), 0, 1),
        "prompt_read": draw_prompt_read(jax.random.fold_in(key_of[11], 71), 0),
        "kl_pair": draw_kl_pair(jax.random.fold_in(key_of[11], 71), 0),
        "kl_ref": draw_kl_ref(jax.random.fold_in(key_of[11], 71), 0),
    }


routed_scale = 16.0
kto_beta = 0.1
loss_scale = 1024.0


def silu_slope(pre_act):
    logistic = jax.nn.sigmoid(pre_act)
    return logistic * (1.0 + pre_act * (1.0 - logistic))


def contract_rows(left, right):
    return lax.dot_general(left, right, (((0,), (0,)), ((), ())), preferred_element_type=jnp.float32)


def reference(tokens, router, expert_ids, w_up, w_down, readout, ref_logp, labels, prompt_read, kl_pair, kl_ref):
    block_total = N_DP * N_EXPERT
    per_expert = block_total * CAP
    logits = jnp.dot(tokens, router, preferred_element_type=jnp.float32)
    scores = jnp.exp(logits)
    router_probs = scores / jnp.sum(scores, axis=1, keepdims=True)
    gate_values = routed_scale * jnp.take_along_axis(router_probs, expert_ids, axis=1)
    blocked = expert_ids.reshape(block_total, TOK_DEV, TOPK)
    onehot = (blocked[..., None] == jnp.arange(EXPERTS, dtype=jnp.int32)).astype(jnp.int32)
    per_token = jnp.sum(onehot, axis=2)
    before = jnp.cumsum(per_token, axis=1) - per_token
    slot_rank = jnp.sum(onehot * before[:, :, None, :], axis=3)
    block_index = jnp.arange(block_total, dtype=jnp.int32)[:, None, None]
    sentinel = EXPERTS * per_expert
    destination = jnp.where(slot_rank < CAP, blocked * per_expert + block_index * CAP + slot_rank, sentinel).astype(jnp.int32)
    token_index = jnp.broadcast_to(jnp.arange(TOKENS, dtype=jnp.int32).reshape(block_total, TOK_DEV, 1), destination.shape)
    slot_token = jnp.full((sentinel + 1,), TOKENS, jnp.int32).at[destination.reshape(-1)].set(token_index.reshape(-1))
    slot_token = slot_token[:sentinel].reshape(EXPERTS, per_expert)
    slot_gate = jnp.zeros((sentinel + 1,), jnp.float32).at[destination.reshape(-1)].set(gate_values.reshape(-1))
    slot_gate = slot_gate[:sentinel].reshape(EXPERTS, per_expert)
    padded_tokens = jnp.concatenate([tokens, jnp.zeros((1, D), tokens.dtype)], axis=0)

    def forward_expert(routed_sum, packed):
        rows_index, rows_gate, up_matrix, down_matrix = packed
        slot_inputs = padded_tokens[rows_index]
        pre_act = jnp.dot(slot_inputs, up_matrix, preferred_element_type=jnp.float32)
        hidden = jax.nn.silu(pre_act).astype(jnp.bfloat16)
        expert_out = jnp.dot(hidden, down_matrix, preferred_element_type=jnp.float32).astype(jnp.bfloat16)
        routed_sum = routed_sum.at[rows_index].add(rows_gate[:, None] * expert_out.astype(jnp.float32))
        return routed_sum, None

    routed_sum, unused = lax.scan(forward_expert, jnp.zeros((TOKENS + 1, D), jnp.float32), (slot_token, slot_gate, w_up, w_down))
    layer_out = tokens.astype(jnp.float32) + routed_sum[:TOKENS]
    token_terms = jnp.sum(layer_out * readout.astype(jnp.float32), axis=1) - ref_logp
    margins = jnp.sum(token_terms.reshape(EXAMPLES, SEQ), axis=1)
    seq_sums = jnp.sum(layer_out.reshape(EXAMPLES, SEQ, D), axis=1)
    example_index = jnp.arange(EXAMPLES, dtype=jnp.int32)
    paired = ((example_index // GROUP_EX) * GROUP_EX + kl_pair).astype(jnp.int32)
    kl_terms = jnp.sum(seq_sums[paired] * prompt_read.astype(jnp.float32), axis=1) - kl_ref
    anchor = jnp.sum(kl_terms) / EXAMPLES
    signed = jnp.where(labels == 1, 1.0, -1.0)
    kept_share = jax.nn.sigmoid(kto_beta * signed * (margins - anchor))
    losses = 1.0 - kept_share
    margin_grad = -loss_scale * kto_beta * signed * kept_share * (1.0 - kept_share)
    grad_layer = jnp.repeat(margin_grad, SEQ)[:, None] * readout.astype(jnp.float32)
    padded_grad = jnp.concatenate([grad_layer, jnp.zeros((1, D), grad_layer.dtype)], axis=0)

    def backward_expert(carried, packed):
        rows_index, rows_gate, up_matrix, down_matrix = packed
        slot_inputs = padded_tokens[rows_index]
        pre_act = jnp.dot(slot_inputs, up_matrix, preferred_element_type=jnp.float32)
        hidden = jax.nn.silu(pre_act).astype(jnp.bfloat16)
        slot_grad = (rows_gate[:, None] * padded_grad[rows_index]).astype(jnp.bfloat16)
        back = lax.dot_general(slot_grad, down_matrix, (((1,), (1,)), ((), ())), preferred_element_type=jnp.float32)
        pre_grad = (back * silu_slope(pre_act)).astype(jnp.bfloat16)
        share_rows = N_EXPERT * CAP
        up_total = jnp.zeros((D, FH), jnp.float32)
        down_total = jnp.zeros((FH, D), jnp.float32)
        for replica in range(N_DP):
            first_row = replica * share_rows
            last_row = first_row + share_rows
            part_up = contract_rows(slot_inputs[first_row:last_row], pre_grad[first_row:last_row]).astype(jnp.bfloat16)
            part_down = contract_rows(hidden[first_row:last_row], slot_grad[first_row:last_row]).astype(jnp.bfloat16)
            up_total = up_total + lax.optimization_barrier(part_up).astype(jnp.float32)
            down_total = down_total + lax.optimization_barrier(part_down).astype(jnp.float32)
        return carried, (up_total.astype(jnp.bfloat16), down_total.astype(jnp.bfloat16))

    unused, grads = lax.scan(backward_expert, jnp.zeros((), jnp.float32), (slot_token, slot_gate, w_up, w_down))
    return (grads[0], grads[1], losses, kl_terms)
```

```python
import jax
import jax.numpy as jnp
from jax import lax
from jax.sharding import PartitionSpec as P

routed_scale = 16.0
kto_beta = 0.1
loss_scale = 1024.0
LANES = 128


def split3(value):
    high = value.astype(jnp.bfloat16)
    rest = value - high.astype(jnp.float32)
    middle = rest.astype(jnp.bfloat16)
    low = (rest - middle.astype(jnp.float32)).astype(jnp.bfloat16)
    return high, middle, low


def contract_rows(left, right):
    return lax.dot_general(
        left, right, (((0,), (0,)), ((), ())), preferred_element_type=jnp.float32
    )


def local(
    tokens,
    router,
    expert_ids,
    w_up,
    w_down,
    readout,
    ref_logp,
    labels,
    prompt_read,
    kl_pair,
    kl_ref,
):
    f32, bf16 = jnp.float32, jnp.bfloat16
    experts = lax.axis_size("expert")
    replicas = lax.axis_size("dp")
    group = lax.axis_index("dp")
    me = lax.axis_index("expert")
    tok_rows, width = tokens.shape
    top_count = expert_ids.shape[1]
    capacity = 4 * tok_rows * top_count // (5 * experts)
    up_matrix = w_up[0]
    down_matrix = w_down[0]
    share = width // experts
    rows = capacity + 1

    logits = jnp.dot(tokens, router, preferred_element_type=f32)
    scores = jnp.exp(logits)
    probs = scores / jnp.sum(scores, axis=1, keepdims=True)
    gates = routed_scale * probs[:, :experts]

    named = jnp.any(
        expert_ids[:, :, None] == jnp.arange(experts, dtype=jnp.int32)[None, None, :], axis=1
    )
    named_f = named.astype(f32)
    tri = (jnp.arange(tok_rows)[:, None] > jnp.arange(tok_rows)[None, :]).astype(bf16)
    rank = jnp.dot(tri, named_f.astype(bf16), preferred_element_type=f32).astype(jnp.int32)
    place = jnp.where(named & (rank < capacity), rank, rows)
    pick = (place.T[:, None, :] == jnp.arange(rows, dtype=jnp.int32)[None, :, None])
    slot_gate = jnp.sum(jnp.where(pick, gates.T[:, None, :], 0.0), axis=2)
    pick = pick.astype(bf16)

    tokens_f = tokens.astype(f32)
    readout_f = readout.astype(f32)
    own_margin = jnp.sum(tokens_f * readout_f) - jnp.sum(ref_logp)
    base = jnp.sum(tokens_f, axis=0).reshape(experts, share)

    sent_x = lax.dot_general(pick, tokens, (((2,), (0,)), ((), ())), preferred_element_type=f32).astype(bf16)
    sent_y = lax.dot_general(pick, readout, (((2,), (0,)), ((), ())), preferred_element_type=f32).astype(bf16)
    last = jnp.concatenate(split3(base) + (jnp.zeros((experts, width - 3 * share), bf16),), axis=1)
    is_last = (jnp.arange(rows) == capacity)[None, :, None]
    sent_x = jnp.where(is_last, last[:, None, :], sent_x)
    sent_y = jnp.where(is_last, prompt_read[0][None, None, :], sent_y)
    pair_column = jnp.where(is_last[:, :, 0], kl_pair[0].astype(f32), slot_gate)
    extra = jnp.stack(split3(pair_column), axis=2)
    extra = jnp.pad(extra, ((0, 0), (0, 0), (0, LANES - 3)))
    sent = jnp.concatenate([sent_x, sent_y, extra], axis=2)
    got = lax.all_to_all(sent, "expert", split_axis=0, concat_axis=0, tiled=True)

    got_gate = jnp.sum(got[:, :, 2 * width : 2 * width + 3].astype(f32), axis=2)
    pair_of = got_gate[:, capacity].astype(jnp.int32)
    gate = jnp.where(jnp.arange(rows)[None, :] == capacity, 0.0, got_gate).reshape(-1, 1)
    x = got[:, :, :width].reshape(experts * rows, width)
    y = got[:, :, width : 2 * width].reshape(experts * rows, width)
    pre_act = jnp.dot(x, up_matrix, preferred_element_type=f32)
    back = lax.dot_general(y, down_matrix, (((1,), (1,)), ((), ())), preferred_element_type=f32)
    logistic = jax.nn.sigmoid(pre_act)
    hidden = pre_act * logistic
    slope = logistic * (1.0 + pre_act * (1.0 - logistic))
    gated = gate * hidden
    margin_part = jnp.sum((gated * back).reshape(experts, -1), axis=1)
    hidden_sum = jnp.sum(gated.reshape(experts, rows, -1), axis=1)
    prompt_down = back.reshape(experts, rows, -1)[:, capacity]
    base_part = jnp.sum(got[:, capacity, : 3 * share].astype(f32).reshape(experts, 3, share), axis=1)
    prompt_part = lax.dynamic_slice_in_dim(got[:, capacity, width : 2 * width], me * share, share, 1).astype(f32)
    pair_hot = (pair_of[:, None] == jnp.arange(experts)[None, :]).astype(f32)
    kl_matrix = lax.dot_general(
        jnp.concatenate([prompt_down, prompt_part], axis=1),
        jnp.concatenate([hidden_sum, base_part], axis=1),
        (((1,), (1,)), ((), ())),
        precision=lax.Precision.HIGHEST,
        preferred_element_type=f32,
    )
    kl_part = jnp.sum(kl_matrix * pair_hot, axis=1)
    own = jnp.arange(experts) == me
    margin_part = margin_part + jnp.where(own, own_margin, 0.0)
    kl_part = kl_part - jnp.where(own, kl_ref[0], 0.0)
    label_part = jnp.where(own, jnp.where(labels[0] == 1, 1.0, -1.0), 0.0)
    mine = jnp.stack([margin_part, kl_part, label_part])
    spread = jnp.where(jnp.arange(replicas)[:, None, None] == group, mine[None], 0.0)
    total = lax.psum(spread.reshape(-1), ("dp", "expert")).reshape(replicas, 3, experts)
    anchor = jnp.sum(total[:, 1]) / (experts * replicas)
    here = lax.dynamic_index_in_dim(total, group, 0, keepdims=False)
    margins, kl_all, signed = here[0], here[1], here[2]
    kept = jax.nn.sigmoid(kto_beta * signed * (margins - anchor))
    margin_grad = -loss_scale * kto_beta * signed * kept * (1.0 - kept)
    losses = lax.dynamic_slice_in_dim(1.0 - kept, me, 1)
    kl_terms = lax.dynamic_slice_in_dim(kl_all, me, 1)

    row_grad = jnp.broadcast_to(margin_grad[:, None], (experts, rows)).reshape(-1, 1)
    pre_grad = (gate * row_grad * back * slope).astype(bf16)
    scaled = (gated * row_grad).astype(bf16)
    up_part = contract_rows(x, pre_grad).astype(bf16)
    down_part = contract_rows(scaled, y).astype(bf16)
    grad_up = lax.psum_scatter(up_part, "dp", scatter_dimension=0, tiled=True)[None]
    grad_down = lax.psum_scatter(down_part, "dp", scatter_dimension=1, tiled=True)[None]
    return (grad_up, grad_down, losses, kl_terms)


def solution(mesh):
    return jax.shard_map(
        local,
        mesh=mesh,
        in_specs=(
            P(("dp", "expert"), None),
            P(),
            P(("dp", "expert"), None),
            P("expert", None, None),
            P("expert", None, None),
            P(("dp", "expert"), None),
            P(("dp", "expert")),
            P(("dp", "expert")),
            P(("dp", "expert"), None),
            P(("dp", "expert")),
            P(("dp", "expert")),
        ),
        out_specs=(
            P("expert", "dp", None),
            P("expert", None, "dp"),
            P(("dp", "expert")),
            P(("dp", "expert")),
        ),
        check_vma=False,
    )
```

```python
import functools

import jax
import jax.numpy as jnp
from jax import lax
from jax.experimental import pallas as pl
from jax.experimental.pallas import tpu as pltpu
from jax.sharding import PartitionSpec as P

MESH = pl.DeviceIdType.MESH
routed_scale = 16.0
kto_beta = 0.1
loss_scale = 1024.0
f32, bf16 = jnp.float32, jnp.bfloat16

RING = 4
COLUMNS = 16
LANES = 128
META = 80
NT = (((1,), (1,)), ((), ()))
TN = (((0,), (0,)), ((), ()))


def split3(value):
    high = value.astype(bf16).astype(f32)
    middle = (value - high).astype(bf16).astype(f32)
    low = (value - high - middle).astype(bf16).astype(f32)
    return high, middle, low


def place():
    dp, ex = lax.axis_index("dp"), lax.axis_index("expert")
    return dp // 2, dp % 2, ex % 2, ex // 2


def kernel(
    cap, hw, tok, rdo, meta, own, wu_hbm, wd_hbm,
    up_out, down_out, small_out,
    xb, yb, mb, ob, xin, yin, wu, wd, pa, ra, pas, pap, ras, rap, prs, hst, wst,
    exty, hst_t, gsd, grd, acc, arb, arc,
    lsem, ag_s, ag_r, xs, xr, ys, yr, ps, pr, qs, qr, ar_s, ar_r, c_s, c_r, g_s, g_r,
):
    rb = META
    tr = tok.shape[0]
    hid = wu.shape[1]
    x_lo, core, x_hi, col = place()
    dp, ex = lax.axis_index("dp"), lax.axis_index("expert")
    x = x_hi * 2 + x_lo
    y, z = col % RING, col // RING

    def dev_x(xx):
        return ((xx % 2) * 2 + core, col * 2 + xx // 2)

    def dev_col(cc):
        return (dp, cc * 2 + x_hi)

    sibling = (x_lo * 2 + 1 - core, ex)
    partner = ((1 - x_lo) * 2 + core, ex)

    def column_at(k):
        return ((z + k // RING) % RING) * RING + (y + k % RING) % RING

    def column_from(k):
        return ((z + RING - k // RING) % RING) * RING + (y + RING - k % RING) % RING

    def rows_of(cc):
        return pl.ds(pl.multiple_of(cc * rb, 16), rb)

    def tail_of(cc):
        return pl.ds(pl.multiple_of(cc * rb + 64, 16), 16)

    def remote(src, dst, ss, rs, dev):
        return pltpu.make_async_remote_copy(
            src_ref=src, dst_ref=dst, send_sem=ss, recv_sem=rs, device_id=dev, device_id_type=MESH
        )

    barrier = pltpu.get_barrier_semaphore()
    for d in range(1, RING):
        pl.semaphore_signal(barrier, inc=1, device_id=dev_x((x + d) % RING), device_id_type=MESH)

    def greet(k, carry):
        pl.semaphore_signal(barrier, inc=1, device_id=dev_col(column_at(k)), device_id_type=MESH)
        return carry

    lax.fori_loop(1, COLUMNS, greet, 0)
    pl.semaphore_signal(barrier, inc=1, device_id=sibling, device_id_type=MESH)
    half = pl.ds(pl.multiple_of(x_lo * hw, LANES), hw)
    mine = pl.ds(pl.multiple_of(x * tr, LANES), tr)
    locals_ = [
        pltpu.make_async_copy(tok.at[:, half], xb.at[mine], lsem.at[0]),
        pltpu.make_async_copy(rdo.at[:, half], yb.at[mine], lsem.at[1]),
        pltpu.make_async_copy(meta.at[x], mb.at[x], lsem.at[2]),
        pltpu.make_async_copy(wu_hbm.at[half], wu, lsem.at[3]),
        pltpu.make_async_copy(wd_hbm.at[:, half], wd.at[pl.ds(0, hid)], lsem.at[4]),
    ]
    for copy in locals_:
        copy.start()
    pl.semaphore_wait(barrier, RING - 1 + COLUMNS - 1 + 1)

    def ring_copy(which, d):
        to = (x + d) % RING
        cols = pl.ds(pl.multiple_of((to % 2) * hw, LANES), hw)
        src = (meta.at[to], tok.at[:, cols], rdo.at[:, cols])[which]
        dst = (mb.at[x], xb.at[mine], yb.at[mine])[which]
        return remote(src, dst, ag_s.at[which * 3 + d - 1], ag_r.at[which * 3 + d - 1], dev_x(to))

    sends = [ring_copy(which, d) for which in (0, 1) for d in (1, 3, 2)]
    for copy in sends:
        copy.start()
    for copy in sends:
        copy.wait_recv()
    later = [ring_copy(2, d) for d in (1, 3, 2)]
    for copy in later:
        copy.start()
    for copy in locals_:
        copy.wait()

    exty[...] = jnp.zeros_like(exty)
    base_rows = [[], []]
    for j in range(hw // LANES):
        lane = pl.ds(j * LANES, LANES)
        for b in range(RING):
            exty[12 + b : 13 + b, lane] = mb[b, 32 + j : 33 + j, :]
    tall = lax.broadcasted_iota(jnp.int32, (LANES, LANES), 0)
    for j in range(hw // LANES):
        lane = pl.ds(j * LANES, LANES)
        terms = split3(mb[x, 52 + j : 53 + j, :]) + split3(mb[x + 1 - 2 * x_lo, 52 + j : 53 + j, :])
        block = jnp.zeros((LANES, LANES), f32)
        for i, term in enumerate(terms):
            block = jnp.where(tall == i, term, block)
        wd[pl.ds(hid, LANES), lane] = block.astype(bf16)

    wide = 512

    def picks(cc):
        want = jnp.concatenate([mb[b, pl.ds(cc, 1), :] for b in range(RING)], axis=1)
        row = lax.broadcasted_iota(jnp.int32, (LANES, RING * tr), 0).astype(f32)
        return jnp.where(row == want, 1.0, 0.0).astype(bf16)

    def x_copy(k):
        to = column_at(k)
        return remote(ob.at[rows_of(to)], xin.at[rows_of(col)], xs.at[k], xr.at[k], dev_col(to))

    def y_copy(k):
        to = column_at(k)
        return remote(ob.at[rows_of(to)], yin.at[rows_of(col)], ys.at[k], yr.at[k], dev_col(to))

    def build(cc, src, dst, extra):
        pick = picks(cc)
        for j in range(hw // wide):
            lane = pl.ds(j * wide, wide)
            block = jnp.dot(pick[:rb], src[:, lane], preferred_element_type=f32)
            dst[rows_of(cc), lane] = block.astype(bf16)
            tail = extra(j, pick, block[64:rb])
            if tail is not None:
                dst[tail_of(cc), lane] = tail.astype(bf16)

    def x_extra(cc):
        def extra(j, pick, tail):
            if j:
                return None
            gate = jnp.concatenate([mb[b, pl.ds(16 + cc, 1), :] for b in range(RING)], axis=1)
            row = lax.broadcasted_iota(jnp.int32, (16, RING * tr), 0)
            lifted = jnp.zeros((16, RING * tr), f32)
            for i, term in enumerate(split3(gate)):
                lifted = jnp.where(row == 12 + i, term, lifted)
            gates = lax.dot_general(lifted.astype(bf16), pick, NT, preferred_element_type=f32)
            pair = [sum(mb[b, 72 + i : 73 + i, :] for b in range(RING)) for i in range(2)]
            pair = jnp.concatenate(pair + [jnp.zeros((1, wide - 2 * LANES), f32)], axis=1)
            last = lax.broadcasted_iota(jnp.int32, (16, wide), 0) == 15
            gates = jnp.concatenate([gates, jnp.zeros((16, wide - LANES), f32)], axis=1)
            return tail + gates + jnp.where(last, pair, 0.0)

        return extra

    def y_extra(j, pick, tail):
        return tail + exty[:, pl.ds(j * wide, wide)]

    def send_x(k, carry):
        to = column_at(k)
        build(to, xb, ob, x_extra(to))
        x_copy(k).start()
        return carry

    lax.fori_loop(1, COLUMNS, send_x, 0)
    build(col, xb, xin, x_extra(col))
    for copy in later:
        copy.wait_recv()

    def send_y(k, carry):
        to = column_at(k)
        x_copy(k).wait_send()
        build(to, yb, ob, y_extra)
        y_copy(k).start()
        return carry

    lax.fori_loop(1, COLUMNS, send_y, 0)
    build(col, yb, yin, y_extra)

    def pair_x(k):
        at = rows_of(column_from(k))
        return remote(pas.at[at], pap.at[at], ps.at[k], pr.at[k], partner)

    def pair_y(k):
        at = rows_of(column_from(k))
        return remote(ras.at[at], rap.at[at], qs.at[k], qr.at[k], partner)

    def use_x(k, carry):
        at = rows_of(column_from(k))

        @pl.when(k > 0)
        def _():
            x_copy(k).wait_recv()

        part = jnp.dot(xin[at, :], wu[...], preferred_element_type=f32)
        pa[at, :] = part
        pas[at, :] = part.astype(bf16)
        pair_x(k).start()
        return carry

    lax.fori_loop(0, COLUMNS, use_x, 0)

    lane256 = lax.broadcasted_iota(jnp.int32, (rb, 2 * LANES), 1)
    row256 = lax.broadcasted_iota(jnp.int32, (rb, 2 * LANES), 0)
    row_lane = jnp.where(row256 < RING * cap, 12 + row256 // cap, -1)

    def block_of(cc):
        return lane256 - cc * 16 == row_lane

    acc[...] = own[...]

    def meet(k):
        cc = column_from(k)
        at = rows_of(cc)
        pair_x(k).wait_recv()
        pair_y(k).wait_recv()
        p = pa[at, :] + pap[at, :].astype(f32)
        r = ra[at, :] + rap[at, :].astype(f32)
        gate = jnp.sum(xin[tail_of(cc), pl.ds(0, LANES)].astype(f32)[12:15], axis=0, keepdims=True)
        square = lax.broadcasted_iota(jnp.int32, (rb, LANES), 0) == lax.broadcasted_iota(
            jnp.int32, (rb, LANES), 1
        )
        gate = jnp.sum(jnp.where(square, gate, 0.0), axis=1, keepdims=True)
        logistic = jax.nn.sigmoid(p)
        gated = gate * (p * logistic)
        prs[pl.ds(pl.multiple_of(cc * 16, 16), 16), :] = r[64:rb]
        pa[at, :] = gated
        ra[at, :] = gate * r * (logistic * (1.0 + p * (1.0 - logistic)))
        margin = jnp.sum(gated * r, axis=1, keepdims=True)
        hot = jnp.where(block_of(cc), 1.0, 0.0)
        acc[1:2, :] += 0.5 * jnp.sum(hot * margin, axis=0, keepdims=True)
        acc[3:4, :] += xin[tail_of(cc), pl.ds(0, 2 * LANES)].astype(f32)[15:16]
        first = lax.broadcasted_iota(jnp.int32, (16, rb), 0)
        which = lax.broadcasted_iota(jnp.int32, (16, rb), 1) // cap
        rows = jnp.where(first == which, 1.0, 0.0).astype(bf16)
        hst[pl.ds(pl.multiple_of(cc * 16, 16), 16), :] = jnp.dot(
            rows, gated.astype(bf16), preferred_element_type=f32
        )

    lag = 2

    def use_y(k, carry):
        cc = column_from(k)
        at = rows_of(cc)

        @pl.when(k > 0)
        def _():
            y_copy(k).wait_recv()

        part = lax.dot_general(yin[at, :], wd[...], NT, preferred_element_type=f32)
        ra[at, :] = part[:, :hid]
        ras[at, :] = part[:, :hid].astype(bf16)
        wst[pl.ds(pl.multiple_of(cc * 16, 16), 16), :] = part[64:rb, hid:]
        pair_y(k).start()

        @pl.when(k >= lag)
        def _():
            meet(k - lag)

        return carry

    lax.fori_loop(0, COLUMNS, use_y, 0)

    def finish(k, carry):
        meet(k)
        return carry

    lax.fori_loop(COLUMNS - lag, COLUMNS, finish, 0)

    def drain(k, carry):
        pair_x(k).wait_send()
        pair_y(k).wait_send()

        @pl.when(k > 0)
        def _():
            y_copy(k).wait_send()

        return carry

    wide_t = wst[...].T
    base_own = wide_t[0:1] + wide_t[1:2] + wide_t[2:3]
    base_other = wide_t[3:4] + wide_t[4:5] + wide_t[5:6]
    pairs = acc[3:4, :]
    terms = 0.5 * lax.dot_general(
        hst[...], prs[...], NT, precision=lax.Precision.HIGHEST, preferred_element_type=f32
    )
    named = lax.broadcasted_iota(jnp.int32, terms.shape, 0)
    terms += jnp.where(named == col * 16 + x, base_own, 0.0)
    terms += jnp.where(named == col * 16 + x + 1 - 2 * x_lo, base_other, 0.0)
    used = lax.broadcasted_iota(jnp.int32, (1, 2 * LANES), 1) % 16 >= 12
    chosen = jnp.where((named.astype(f32) == pairs) & used, terms, 0.0)
    acc[0:1, :] += jnp.sum(chosen, axis=0, keepdims=True)

    def ring_sum(axis, dev):
        copies = [
            remote(acc, arb.at[axis * 3 + d - 1], ar_s.at[axis * 3 + d - 1], ar_r.at[axis * 3 + d - 1], dev(d))
            for d in (1, 3, 2)
        ]
        for copy in copies:
            copy.start()
        for copy in copies:
            copy.wait()
        acc[...] = acc[...] + arb[axis * 3] + arb[axis * 3 + 1] + arb[axis * 3 + 2]

    ring_sum(0, lambda d: dev_x((x + d) % RING))
    ring_sum(1, lambda d: dev_col(z * RING + (y + d) % RING))
    ring_sum(2, lambda d: dev_col(((z + d) % RING) * RING + y))
    lax.fori_loop(0, COLUMNS, drain, 0)
    for copy in sends + later:
        copy.wait_send()
    swap = remote(acc, arc, c_s.at[0], c_r.at[0], sibling)
    swap.start()
    swap.wait()
    kl_row = jnp.where(used, acc[0:1, :], 0.0)
    kl_other = jnp.where(used, arc[0:1, :], 0.0)
    count = RING * COLUMNS * 2
    anchor = jnp.sum(kl_row + kl_other, axis=1, keepdims=True) / count
    signed = acc[2:3, :]
    kept = jax.nn.sigmoid(kto_beta * signed * (acc[1:2, :] - anchor))
    slope = -loss_scale * kto_beta * signed * kept * (1.0 - kept)
    small_out[...] = jnp.zeros_like(small_out)
    small_out[0:1, :] = 1.0 - kept
    small_out[1:2, :] = kl_row

    def scale(cc, carry):
        at = rows_of(cc)
        factor = jnp.sum(jnp.where(block_of(cc), slope, 0.0), axis=1, keepdims=True)
        pas[at, :] = (pa[at, :] * factor).astype(bf16)
        ras[at, :] = (ra[at, :] * factor).astype(bf16)
        return carry

    lax.fori_loop(0, COLUMNS, scale, 0)
    for j in range(5):
        at = pl.ds(j * 256, 256)
        hst_t[:, at] = pas[at, :].T

    quarter = hw // 2
    step = 256
    other = (1 - core) * quarter
    this = core * quarter

    def up_block(start, j):
        at = pl.ds(pl.multiple_of(start + j * step, LANES), step)
        return lax.dot_general(xin[:, at], ras[...], TN, preferred_element_type=f32)

    def down_block(start, j):
        at = pl.ds(pl.multiple_of(start + j * step, LANES), step)
        return jnp.dot(hst_t[...], yin[:, at], preferred_element_type=f32)

    def piece(j):
        return pl.ds(pl.multiple_of(j * step, step), step)

    def other_up(j, carry):
        pap[piece(j), :] = up_block(other, j).astype(bf16)
        return carry

    def other_down(j, carry):
        gsd[:, piece(j)] = down_block(other, j).astype(bf16)
        return carry

    def this_up(j, carry):
        up_out[piece(j), :] = (up_block(this, j) + rap[piece(j), :].astype(f32)).astype(bf16)
        return carry

    def this_down(j, carry):
        down_out[:, piece(j)] = (down_block(this, j) + grd[:, piece(j)].astype(f32)).astype(bf16)
        return carry

    up_copy = remote(pap, rap, g_s.at[0], g_r.at[0], sibling)
    down_copy = remote(gsd, grd, g_s.at[1], g_r.at[1], sibling)
    lax.fori_loop(0, quarter // step, other_up, 0)
    up_copy.start()
    lax.fori_loop(0, quarter // step, other_down, 0)
    down_copy.start()
    up_copy.wait_recv()
    lax.fori_loop(0, quarter // step, this_up, 0)
    down_copy.wait_recv()
    lax.fori_loop(0, quarter // step, this_down, 0)
    up_copy.wait_send()
    down_copy.wait_send()


def local(
    tokens, router, expert_ids, w_up, w_down, readout, ref_logp, labels, prompt_read, kl_pair, kl_ref
):
    experts = lax.axis_size("expert")
    tr, width = tokens.shape
    top = expert_ids.shape[1]
    cap = 4 * tr * top // (5 * experts)
    hid = w_up.shape[2]
    hw = width // 2
    x_lo, core, x_hi, col = place()
    x = x_hi * 2 + x_lo

    logits = jnp.dot(tokens, router, preferred_element_type=f32)
    scores = jnp.exp(logits)
    gates = routed_scale * (scores / jnp.sum(scores, axis=1, keepdims=True))[:, :experts]
    named = jnp.any(expert_ids[:, :, None] == jnp.arange(experts, dtype=jnp.int32), axis=1)
    before = (jnp.arange(tr)[:, None] > jnp.arange(tr)[None, :]).astype(bf16)
    rank = jnp.dot(before, named.astype(bf16), preferred_element_type=f32)
    want = jnp.where(named & (rank < cap), rank + (cap * x).astype(f32), -1.0)
    by_expert = jnp.stack([want, gates]).transpose(2, 0, 1).reshape(COLUMNS, 2, 2, tr)
    by_expert = by_expert.transpose(1, 2, 0, 3).reshape(2, 2 * COLUMNS, tr)

    tokens_f = tokens.astype(f32)
    own_margin = jnp.sum(tokens_f * readout.astype(f32)) - jnp.sum(ref_logp)
    base = jnp.sum(tokens_f, axis=0).reshape(2, hw // LANES, LANES)
    prompt = prompt_read.astype(f32).reshape(2, hw // LANES, LANES)
    lane = jnp.arange(2 * LANES)
    spot = lane == col * 16 + 12 + x
    pair = (kl_pair[0] // 2) * 16 + (kl_pair[0] % 2) * 2 + x_lo
    misc = jnp.pad(jnp.where(spot, pair, 0).astype(f32).reshape(2, LANES), ((0, 6), (0, 0)))
    per_half = jnp.concatenate([prompt, base], axis=1)
    meta = jnp.concatenate(
        [
            jnp.repeat(by_expert, 2, axis=0),
            jnp.concatenate([per_half, per_half], axis=0),
            jnp.broadcast_to(misc, (RING, 8, LANES)),
        ],
        axis=1,
    )
    sign = jnp.where(labels[0] == 1, 1.0, -1.0)
    own = jnp.where(spot[None, :], jnp.stack([-kl_ref[0], own_margin, sign])[:, None], 0.0)
    own = jnp.pad(own, ((0, 5), (0, 0)))

    slots = COLUMNS * META
    quarter = hw // 2
    dma = pltpu.SemaphoreType.DMA
    any_ = pl.BlockSpec(memory_space=pl.ANY)
    vmem = pl.BlockSpec(memory_space=pltpu.VMEM)
    up, down, small = pl.pallas_call(
        functools.partial(kernel, cap, hw),
        out_shape=(
            jax.ShapeDtypeStruct((quarter, hid), bf16),
            jax.ShapeDtypeStruct((hid, quarter), bf16),
            jax.ShapeDtypeStruct((8, 2 * LANES), f32),
        ),
        in_specs=[any_, any_, any_, vmem, any_, any_],
        out_specs=(vmem, vmem, vmem),
        scratch_shapes=[
            pltpu.VMEM((RING * tr, hw), bf16),
            pltpu.VMEM((RING * tr, hw), bf16),
            pltpu.VMEM((RING, META, LANES), f32),
            pltpu.VMEM((slots, hw), bf16),
            pltpu.VMEM((slots, hw), bf16),
            pltpu.VMEM((slots, hw), bf16),
            pltpu.VMEM((hw, hid), bf16),
            pltpu.VMEM((hid + LANES, hw), bf16),
            pltpu.VMEM((slots, hid), f32),
            pltpu.VMEM((slots, hid), f32),
            pltpu.VMEM((slots, hid), bf16),
            pltpu.VMEM((slots, hid), bf16),
            pltpu.VMEM((slots, hid), bf16),
            pltpu.VMEM((slots, hid), bf16),
            pltpu.VMEM((COLUMNS * 16, hid), f32),
            pltpu.VMEM((COLUMNS * 16, hid), f32),
            pltpu.VMEM((COLUMNS * 16, LANES), f32),
            pltpu.VMEM((16, hw), f32),
            pltpu.VMEM((hid, slots), bf16),
            pltpu.VMEM((hid, quarter), bf16),
            pltpu.VMEM((hid, quarter), bf16),
            pltpu.VMEM((8, 2 * LANES), f32),
            pltpu.VMEM((9, 8, 2 * LANES), f32),
            pltpu.VMEM((8, 2 * LANES), f32),
            dma((5,)),
            dma((9,)), dma((9,)),
            dma((COLUMNS,)), dma((COLUMNS,)),
            dma((COLUMNS,)), dma((COLUMNS,)),
            dma((COLUMNS,)), dma((COLUMNS,)),
            dma((COLUMNS,)), dma((COLUMNS,)),
            dma((9,)), dma((9,)),
            dma((1,)), dma((1,)),
            dma((2,)), dma((2,)),
        ],
        compiler_params=pltpu.CompilerParams(
            collective_id=0, has_side_effects=True, vmem_limit_bytes=63 * 2**20
        ),
        cost_estimate=pl.CostEstimate(flops=40 * 10**9, bytes_accessed=30 * 10**6, transcendentals=10**6),
        name="routed_step",
    )(tokens, readout, meta, own, w_up[0], w_down[0])
    here = col * 16 + 12 + x
    losses = lax.dynamic_slice(small, (0, here), (1, 1)).reshape(1)
    kl_terms = lax.dynamic_slice(small, (1, here), (1, 1)).reshape(1)
    return up[None], down[None], losses, kl_terms


def solution(mesh):
    return jax.shard_map(
        local,
        mesh=mesh,
        in_specs=(
            P(("dp", "expert"), None),
            P(),
            P(("dp", "expert"), None),
            P("expert", None, None),
            P("expert", None, None),
            P(("dp", "expert"), None),
            P(("dp", "expert")),
            P(("dp", "expert")),
            P(("dp", "expert"), None),
            P(("dp", "expert")),
            P(("dp", "expert")),
        ),
        out_specs=(
            P("expert", "dp", None),
            P("expert", None, "dp"),
            P(("dp", "expert")),
            P(("dp", "expert")),
        ),
        check_vma=False,
    )
```

```python
import functools

import jax
import jax.numpy as jnp
from jax import lax
from jax.experimental import pallas as pl
from jax.experimental.pallas import tpu as pltpu
from jax.sharding import PartitionSpec as P

MESH = pl.DeviceIdType.MESH
routed_scale = 16.0
kto_beta = 0.1
loss_scale = 1024.0
f32, bf16 = jnp.float32, jnp.bfloat16

RING = 4
COLUMNS = 16
LANES = 128
META = 80
PARTS = (32, 32, 16)
PART_AT = (0, 32, 64)
NT = (((1,), (1,)), ((), ()))
TN = (((0,), (0,)), ((), ()))


def split3(value):
    high = value.astype(bf16).astype(f32)
    middle = (value - high).astype(bf16).astype(f32)
    low = (value - high - middle).astype(bf16).astype(f32)
    return high, middle, low


def place():
    dp, ex = lax.axis_index("dp"), lax.axis_index("expert")
    return dp // 2, dp % 2, ex % 2, ex // 2


def kernel(
    cap, hw, tok, rdo, meta, own, wu_hbm, wd_hbm,
    up_hbm, down_hbm, small_out,
    xb, yb, mb, ob, xin, yin, m1x, m2x, m1y, m2y, wu, wd, pa, ra, pas, pap, ras, rap, prs, hst, wst,
    exty, acc, arb, arc,
    lsem, osem, ag_s, ag_r, a1s, a1r, a2s, a2r, b1s, b1r, b2s, b2r, ds, dr,
    ps, pr, qs, qr, ar_s, ar_r, c_s, c_r, g_s, g_r,
):
    rb = META
    tr = tok.shape[0]
    hid = wu.shape[1]
    slots = COLUMNS * rb
    x_lo, core, x_hi, col = place()
    dp, ex = lax.axis_index("dp"), lax.axis_index("expert")
    x = x_hi * 2 + x_lo
    y, z = col % RING, col // RING
    mid = hw // 2

    def dev_x(xx):
        return ((xx % 2) * 2 + core, col * 2 + xx // 2)

    def dev_col(cc):
        return (dp, cc * 2 + x_hi)

    sibling = (x_lo * 2 + 1 - core, ex)
    partner = ((1 - x_lo) * 2 + core, ex)

    def plus(dz, dy):
        return ((z + dz) % RING) * RING + (y + dy) % RING

    def minus(dz, dy):
        return ((z + RING - dz) % RING) * RING + (y + RING - dy) % RING

    def rows(start, size):
        return pl.ds(pl.multiple_of(start, 16), size)

    def remote(src, dst, ss, rs, dev):
        return pltpu.make_async_remote_copy(
            src_ref=src, dst_ref=dst, send_sem=ss, recv_sem=rs, device_id=dev, device_id_type=MESH
        )

    def loop(count, body, start=0):
        def step(i, carry):
            body(i)
            return carry

        lax.fori_loop(start, count, step, 0)

    barrier = pltpu.get_barrier_semaphore()

    def greet(dev):
        pl.semaphore_signal(barrier, inc=1, device_id=dev, device_id_type=MESH)

    loop(RING, lambda d: greet(dev_x((x + d) % RING)), 1)
    loop(RING, lambda d: greet(dev_col(plus(d, 0))), 1)
    loop(RING, lambda d: greet(dev_col(plus(0, d))), 1)
    greet(sibling)
    half = pl.ds(pl.multiple_of(x_lo * hw, LANES), hw)
    mine = pl.ds(pl.multiple_of(x * tr, LANES), tr)
    locals_ = [
        pltpu.make_async_copy(tok.at[:, half], xb.at[mine], lsem.at[0]),
        pltpu.make_async_copy(rdo.at[:, half], yb.at[mine], lsem.at[1]),
        pltpu.make_async_copy(meta.at[x], mb.at[x], lsem.at[2]),
        pltpu.make_async_copy(wu_hbm.at[half], wu, lsem.at[3]),
        pltpu.make_async_copy(wd_hbm.at[:, half], wd.at[pl.ds(0, hid)], lsem.at[4]),
    ]
    for copy in locals_:
        copy.start()
    pl.semaphore_wait(barrier, 3 * (RING - 1) + 1)

    pieces = ((0, 0, hw), (1, 0, mid), (1, mid, mid), (2, 0, hw))

    def ring_copy(which, d):
        to = (x + d) % RING
        kind, start, size = pieces[which]
        cols = pl.ds(pl.multiple_of((to % 2) * hw + start, LANES), size)
        here = pl.ds(start, size)
        src = (meta.at[to], tok.at[:, cols], rdo.at[:, cols])[kind]
        dst = (mb.at[x], xb.at[mine, here], yb.at[mine, here])[kind]
        return remote(src, dst, ag_s.at[which * 3 + d - 1], ag_r.at[which * 3 + d - 1], dev_x(to))

    rings = [[ring_copy(which, d) for d in (1, 3, 2)] for which in range(4)]

    def start_ring(which):
        for copy in rings[which]:
            copy.start()

    def wait_ring(which):
        for copy in rings[which]:
            copy.wait_recv()

    start_ring(0)
    start_ring(1)
    for copy in locals_:
        copy.wait()
    wait_ring(0)

    exty[...] = jnp.zeros_like(exty)
    tall = lax.broadcasted_iota(jnp.int32, (LANES, LANES), 0)
    for j in range(hw // LANES):
        lane = pl.ds(j * LANES, LANES)
        for b in range(RING):
            exty[12 + b : 13 + b, lane] = mb[b, 32 + j : 33 + j, :]
        terms = split3(mb[x, 52 + j : 53 + j, :]) + split3(mb[x + 1 - 2 * x_lo, 52 + j : 53 + j, :])
        block = jnp.zeros((LANES, LANES), f32)
        for i, term in enumerate(terms):
            block = jnp.where(tall == i, term, block)
        wd[pl.ds(hid, LANES), lane] = block.astype(bf16)

    def shipment(n):
        if n < 2:
            return rb, 0, n * mid, mid, 0, n * (mid // 2), m1x, m2x, xin
        size, at = PARTS[n - 2], PART_AT[n - 2]
        return size, at * COLUMNS, 0, hw, at * 9, 0, m1y, m2y, yin

    def block(n, cc):
        size, base = shipment(n)[:2]
        return rows(base + cc * size, size)

    def halves(n):
        start, width = shipment(n)[2:4]
        return pl.ds(start, width // 2), pl.ds(start + width // 2, width // 2), pl.ds(start, width)

    def held(n, i):
        size, _, _, width, base, at = shipment(n)[:6]
        return rows(base + i * size, size), pl.ds(at, width // 2)

    def turn(i):
        return 1 + i // 3, 1 + i % 3

    def a_first(n, i):
        dz, dy = turn(i)
        there = held(n, i)
        return remote(
            ob.at[block(n, plus(dz, dy)), halves(n)[0]], shipment(n)[6].at[there[0], there[1]],
            a1s.at[n, i], a1r.at[n, i], dev_col(plus(0, dy)),
        )

    def a_second(n, i):
        dz, dy = turn(i)
        there = held(n, i)
        return remote(
            shipment(n)[6].at[there[0], there[1]], shipment(n)[8].at[block(n, minus(0, dy)), halves(n)[0]],
            a2s.at[n, i], a2r.at[n, i], dev_col(plus(dz, 0)),
        )

    def b_first(n, i):
        dz, dy = turn(i)
        there = held(n, i)
        return remote(
            ob.at[block(n, plus(dz, dy)), halves(n)[1]], shipment(n)[7].at[there[0], there[1]],
            b1s.at[n, i], b1r.at[n, i], dev_col(plus(dz, 0)),
        )

    def b_second(n, i):
        dz, dy = turn(i)
        there = held(n, i)
        return remote(
            shipment(n)[7].at[there[0], there[1]], shipment(n)[8].at[block(n, minus(dz, 0)), halves(n)[1]],
            b2s.at[n, i], b2r.at[n, i], dev_col(plus(0, dy)),
        )

    def straight(n, i):
        dz, dy = (i + 1) * (1 - i // 3), (i - 2) * (i // 3)
        to = plus(dz, dy)
        return remote(
            ob.at[block(n, to), halves(n)[2]], shipment(n)[8].at[block(n, col), halves(n)[2]],
            ds.at[n, i], dr.at[n, i], dev_col(to),
        )

    def keep(n):
        cols = halves(n)[2]
        return pltpu.make_async_copy(ob.at[block(n, col), cols], shipment(n)[8].at[block(n, col), cols], osem.at[n])

    wide = 512

    def picks(cc, start, size):
        want = jnp.concatenate([mb[b, pl.ds(cc, 1), :] for b in range(RING)], axis=1)
        row = start + lax.broadcasted_iota(jnp.int32, (size, RING * tr), 0).astype(f32)
        return jnp.where(row == want, 1.0, 0.0).astype(bf16)

    def gate_rows(cc):
        gate = jnp.concatenate([mb[b, pl.ds(16 + cc, 1), :] for b in range(RING)], axis=1)
        row = lax.broadcasted_iota(jnp.int32, (16, RING * tr), 0)
        lifted = jnp.zeros((16, RING * tr), f32)
        for i, term in enumerate(split3(gate)):
            lifted = jnp.where(row == 12 + i, term, lifted)
        gates = lax.dot_general(lifted.astype(bf16), picks(cc, 0, LANES), NT, preferred_element_type=f32)
        pair = [sum(mb[b, 72 + i : 73 + i, :] for b in range(RING)) for i in range(2)]
        pair = jnp.concatenate(pair, axis=1)
        gates = jnp.concatenate([gates, jnp.zeros((16, LANES), f32)], axis=1)
        last = lax.broadcasted_iota(jnp.int32, (16, 2 * LANES), 0) == 15
        return gates + jnp.where(last, pair, 0.0)

    def build(n):
        size, base, start, width = shipment(n)[:4]
        at = 0 if n < 2 else PART_AT[n - 2]
        source = xb if n < 2 else yb

        def plane(zz):
            pick = jnp.concatenate([picks(zz * RING + i, at, size) for i in range(RING)], axis=0)
            place_ = rows(base + zz * (RING * size), RING * size)
            for lo in range(start, start + width, wide):
                lane = pl.ds(lo, min(wide, start + width - lo))
                made = jnp.dot(pick, source[:, lane], preferred_element_type=f32)
                if n == 4:
                    made = made + jnp.concatenate([exty[:, lane]] * RING, axis=0)
                ob[place_, lane] = made.astype(bf16)
            if n == 0:
                for i in range(RING):
                    tail = rows(zz * (RING * size) + i * size + 64, 16)
                    first = pl.ds(0, 2 * LANES)
                    ob[tail, first] = (ob[tail, first].astype(f32) + gate_rows(zz * RING + i)).astype(bf16)

        def go(k):
            dz = (k + 1) % RING
            plane((z + dz) % RING)

            @pl.when(dz > 0)
            def _():
                for dy in range(1, RING):
                    i = (dz - 1) * 3 + dy - 1
                    a_first(n, i).start()
                    b_first(n, i).start()
                straight(n, dz - 1).start()

            @pl.when(dz == 0)
            def _():
                for dy in range(1, RING):
                    straight(n, 2 + dy).start()
                keep(n).start()

        loop(RING, go)

    def forward(n):
        def go(i):
            a_first(n, i).wait_recv()
            a_second(n, i).start()
            b_first(n, i).wait_recv()
            b_second(n, i).start()

        loop(9, go)

    def built_sent(n):
        def go(i):
            a_first(n, i).wait_send()
            b_first(n, i).wait_send()

        loop(9, go)
        loop(6, lambda i: straight(n, i).wait_send())
        if n < 2:
            keep(n).wait()

    def forwards_sent(n):
        def go(i):
            a_second(n, i).wait_send()
            b_second(n, i).wait_send()

        loop(9, go)

    def arrived(n):
        def go(i):
            a_second(n, i).wait_recv()
            b_second(n, i).wait_recv()

        loop(9, go)
        loop(6, lambda i: straight(n, i).wait_recv())
        if n >= 2:
            keep(n).wait()

    span = 256

    def pair_x(j):
        at = rows(j * span, span)
        return remote(pas.at[at], pap.at[at], ps.at[j], pr.at[j], partner)

    def pair_y(j):
        at = rows(j * span, span)
        return remote(ras.at[at], rap.at[at], qs.at[j], qr.at[j], partner)

    def use_x(j):
        at = rows(j * span, span)
        part = jnp.dot(xin[at, :], wu[...], preferred_element_type=f32)
        pa[at, :] = part
        pas[at, :] = part.astype(bf16)
        pair_x(j).start()

    def use_y(j):
        at = rows(j * span, span)
        part = lax.dot_general(yin[at, :], wd[pl.ds(0, hid), :], NT, preferred_element_type=f32)
        ra[at, :] = part
        ras[at, :] = part.astype(bf16)
        pair_y(j).start()

    acc[...] = own[...]

    def meet(p):
        size, at = PARTS[p], PART_AT[p]
        shape = (size, 2 * LANES)
        lane = lax.broadcasted_iota(jnp.int32, shape, 1)
        row = at + lax.broadcasted_iota(jnp.int32, shape, 0)
        row_lane = jnp.where(row < RING * cap, 12 + row // cap, -1)
        square = at + lax.broadcasted_iota(jnp.int32, (size, LANES), 0) == lax.broadcasted_iota(
            jnp.int32, (size, LANES), 1
        )
        first = lax.broadcasted_iota(jnp.int32, (16, size), 0)
        which = (at + lax.broadcasted_iota(jnp.int32, (16, size), 1)) // cap
        gather = jnp.where(first == which, 1.0, 0.0).astype(bf16)

        def go(cc):
            xr_ = rows(cc * rb + at, size)
            yr_ = rows(at * COLUMNS + cc * size, size)
            tail = xin[rows(cc * rb + 64, 16), pl.ds(0, 2 * LANES)].astype(f32)
            p_ = pa[xr_, :] + pap[xr_, :].astype(f32)
            r = ra[yr_, :] + rap[yr_, :].astype(f32)
            gate = jnp.sum(tail[12:15, :LANES], axis=0, keepdims=True)
            gate = jnp.sum(jnp.where(square, gate, 0.0), axis=1, keepdims=True)
            logistic = jax.nn.sigmoid(p_)
            gated = gate * (p_ * logistic)
            ra[yr_, :] = gated
            pa[xr_, :] = gate * r * (logistic * (1.0 + p_ * (1.0 - logistic)))
            margin = jnp.sum(gated * r, axis=1, keepdims=True)
            hot = jnp.where(lane - cc * 16 == row_lane, 1.0, 0.0)
            acc[1:2, :] += 0.5 * jnp.sum(hot * margin, axis=0, keepdims=True)
            spot = rows(cc * 16, 16)
            summed = jnp.dot(gather, gated.astype(bf16), preferred_element_type=f32)
            if p == 0:
                acc[3:4, :] += tail[15:16]
                hst[spot, :] = summed
            else:
                hst[spot, :] += summed
            if p == 2:
                prs[spot, :] = r

        loop(COLUMNS, go)

    wait_ring(1)
    start_ring(2)
    build(0)
    wait_ring(2)
    start_ring(3)
    build(1)
    forward(0)
    built_sent(0)
    forward(1)
    built_sent(1)
    wait_ring(3)
    build(2)
    build(3)
    arrived(0)
    arrived(1)
    loop(5, use_x)
    forward(2)
    build(4)
    forward(3)
    arrived(2)
    loop(2, use_y)
    forward(4)
    arrived(3)
    loop(4, use_y, 2)
    loop(5, lambda j: pair_x(j).wait_recv())
    loop(2, lambda j: pair_y(j).wait_recv())
    meet(0)
    arrived(4)
    last_at = rows(4 * span, span)
    last_part = lax.dot_general(yin[last_at, :], wd[...], NT, preferred_element_type=f32)
    ra[last_at, :] = last_part[:, :hid]
    ras[last_at, :] = last_part[:, :hid].astype(bf16)
    pair_y(4).start()
    wst[...] = last_part[:, hid:]
    loop(4, lambda j: pair_y(j).wait_recv(), 2)
    meet(1)
    pair_y(4).wait_recv()
    meet(2)

    wide_t = wst[...].T
    base_own = wide_t[0:1] + wide_t[1:2] + wide_t[2:3]
    base_other = wide_t[3:4] + wide_t[4:5] + wide_t[5:6]
    pairs = acc[3:4, :]
    terms = 0.5 * lax.dot_general(
        hst[...], prs[...], NT, precision=lax.Precision.HIGHEST, preferred_element_type=f32
    )
    named = lax.broadcasted_iota(jnp.int32, terms.shape, 0)
    terms += jnp.where(named == col * 16 + x, base_own, 0.0)
    terms += jnp.where(named == col * 16 + x + 1 - 2 * x_lo, base_other, 0.0)
    used = lax.broadcasted_iota(jnp.int32, (1, 2 * LANES), 1) % 16 >= 12
    chosen = jnp.where((named.astype(f32) == pairs) & used, terms, 0.0)
    acc[0:1, :] += jnp.sum(chosen, axis=0, keepdims=True)

    def ring_sum(axis, dev):
        copies = [
            remote(acc, arb.at[axis * 3 + d - 1], ar_s.at[axis * 3 + d - 1], ar_r.at[axis * 3 + d - 1], dev(d))
            for d in (1, 3, 2)
        ]
        for copy in copies:
            copy.start()
        for copy in copies:
            copy.wait()
        acc[...] = acc[...] + arb[axis * 3] + arb[axis * 3 + 1] + arb[axis * 3 + 2]

    ring_sum(0, lambda d: dev_x((x + d) % RING))
    ring_sum(1, lambda d: dev_col(plus(0, d)))
    ring_sum(2, lambda d: dev_col(plus(d, 0)))
    for n in range(2, 5):
        built_sent(n)
    for n in range(5):
        forwards_sent(n)
    loop(5, lambda j: pair_x(j).wait_send())
    loop(5, lambda j: pair_y(j).wait_send())
    for ring in rings:
        for copy in ring:
            copy.wait_send()
    swap = remote(acc, arc, c_s.at[0], c_r.at[0], sibling)
    swap.start()
    swap.wait()
    kl_row = jnp.where(used, acc[0:1, :], 0.0)
    kl_other = jnp.where(used, arc[0:1, :], 0.0)
    count = RING * COLUMNS * 2
    anchor = jnp.sum(kl_row + kl_other, axis=1, keepdims=True) / count
    signed = acc[2:3, :]
    kept = jax.nn.sigmoid(kto_beta * signed * (acc[1:2, :] - anchor))
    slope = -loss_scale * kto_beta * signed * kept * (1.0 - kept)
    small_out[...] = jnp.zeros_like(small_out)
    small_out[0:1, :] = 1.0 - kept
    small_out[1:2, :] = kl_row

    def scaled(source, dst, start, size, at):
        lane = lax.broadcasted_iota(jnp.int32, (size, 2 * LANES), 1)
        row = at + lax.broadcasted_iota(jnp.int32, (size, 2 * LANES), 0)
        row_lane = jnp.where(row < RING * cap, 12 + row // cap, -1)

        def go(cc):
            here = rows(start + cc * size, size)
            factor = jnp.sum(jnp.where(lane - cc * 16 == row_lane, slope, 0.0), axis=1, keepdims=True)
            dst[here, :] = (source[here, :] * factor).astype(bf16)

        loop(COLUMNS, go)

    quarter = hw // 2
    step = 256
    other = (1 - core) * quarter
    this = core * quarter
    hid_t = m2y.at[pl.ds(0, hid)]
    up_got, down_got = rap, m1y.at[pl.ds(0, hid)]
    up_out, down_out = pl.ds(0, hid), m1x.at[pl.ds(0, hid)]
    down_sent = pl.ds(quarter, quarter)

    def up_block(start, j):
        at = pl.ds(pl.multiple_of(start + j * step, LANES), step)
        return lax.dot_general(xin[:, at], pas[...], TN, preferred_element_type=f32)

    def down_block(start, j):
        at = pl.ds(pl.multiple_of(start + j * step, LANES), step)
        return jnp.dot(hid_t[...], yin[:, at], preferred_element_type=f32)

    def piece(j, base=0):
        return pl.ds(pl.multiple_of(base + j * step, step), step)

    def other_up(j):
        pap[piece(j), :] = up_block(other, j).astype(bf16)

    def other_down(j):
        ob[pl.ds(0, hid), piece(j, quarter)] = down_block(other, j).astype(bf16)

    def this_up(j):
        ob[piece(j), up_out] = (up_block(this, j) + up_got[piece(j), :].astype(f32)).astype(bf16)

    def this_down(j):
        down_out[:, piece(j)] = (down_block(this, j) + down_got[:, piece(j)].astype(f32)).astype(bf16)

    up_copy = remote(pap, up_got, g_s.at[0], g_r.at[0], sibling)
    down_copy = remote(ob.at[pl.ds(0, hid), down_sent], down_got, g_s.at[1], g_r.at[1], sibling)
    blocks = quarter // step
    scaled(pa, pas, 0, rb, 0)
    loop(blocks, other_up)
    up_copy.start()
    for p in range(3):
        scaled(ra, ras, PART_AT[p] * COLUMNS, PARTS[p], PART_AT[p])
    for j in range(slots // step):
        at = pl.ds(j * step, step)
        hid_t[:, at] = ras[at, :].T
    loop(blocks, other_down)
    down_copy.start()
    up_copy.wait_recv()
    loop(blocks, this_up)
    up_done = pltpu.make_async_copy(ob.at[pl.ds(0, quarter), up_out], up_hbm, lsem.at[0])
    up_done.start()
    down_copy.wait_recv()
    loop(blocks, this_down)
    down_done = pltpu.make_async_copy(down_out, down_hbm, lsem.at[1])
    down_done.start()
    up_copy.wait_send()
    down_copy.wait_send()
    up_done.wait()
    down_done.wait()


def local(
    tokens, router, expert_ids, w_up, w_down, readout, ref_logp, labels, prompt_read, kl_pair, kl_ref
):
    experts = lax.axis_size("expert")
    tr, width = tokens.shape
    top = expert_ids.shape[1]
    cap = 4 * tr * top // (5 * experts)
    hid = w_up.shape[2]
    hw = width // 2
    x_lo, core, x_hi, col = place()
    x = x_hi * 2 + x_lo

    logits = jnp.dot(tokens, router, preferred_element_type=f32)
    scores = jnp.exp(logits)
    gates = routed_scale * (scores / jnp.sum(scores, axis=1, keepdims=True))[:, :experts]
    named = jnp.any(expert_ids[:, :, None] == jnp.arange(experts, dtype=jnp.int32), axis=1)
    before = (jnp.arange(tr)[:, None] > jnp.arange(tr)[None, :]).astype(bf16)
    rank = jnp.dot(before, named.astype(bf16), preferred_element_type=f32)
    want = jnp.where(named & (rank < cap), rank + (cap * x).astype(f32), -1.0)
    by_expert = jnp.stack([want, gates]).transpose(2, 0, 1).reshape(COLUMNS, 2, 2, tr)
    by_expert = by_expert.transpose(1, 2, 0, 3).reshape(2, 2 * COLUMNS, tr)

    tokens_f = tokens.astype(f32)
    own_margin = jnp.sum(tokens_f * readout.astype(f32)) - jnp.sum(ref_logp)
    base = jnp.sum(tokens_f, axis=0).reshape(2, hw // LANES, LANES)
    prompt = prompt_read.astype(f32).reshape(2, hw // LANES, LANES)
    lane = jnp.arange(2 * LANES)
    spot = lane == col * 16 + 12 + x
    pair = (kl_pair[0] // 2) * 16 + (kl_pair[0] % 2) * 2 + x_lo
    misc = jnp.pad(jnp.where(spot, pair, 0).astype(f32).reshape(2, LANES), ((0, 6), (0, 0)))
    per_half = jnp.concatenate([prompt, base], axis=1)
    meta = jnp.concatenate(
        [
            jnp.repeat(by_expert, 2, axis=0),
            jnp.concatenate([per_half, per_half], axis=0),
            jnp.broadcast_to(misc, (RING, 8, LANES)),
        ],
        axis=1,
    )
    sign = jnp.where(labels[0] == 1, 1.0, -1.0)
    own = jnp.where(spot[None, :], jnp.stack([-kl_ref[0], own_margin, sign])[:, None], 0.0)
    own = jnp.pad(own, ((0, 5), (0, 0)))

    slots = COLUMNS * META
    quarter = hw // 2
    dma = pltpu.SemaphoreType.DMA
    any_ = pl.BlockSpec(memory_space=pl.ANY)
    vmem = pl.BlockSpec(memory_space=pltpu.VMEM)
    up, down, small = pl.pallas_call(
        functools.partial(kernel, cap, hw),
        out_shape=(
            jax.ShapeDtypeStruct((quarter, hid), bf16),
            jax.ShapeDtypeStruct((hid, quarter), bf16),
            jax.ShapeDtypeStruct((8, 2 * LANES), f32),
        ),
        in_specs=[any_, any_, any_, vmem, any_, any_],
        out_specs=(any_, any_, vmem),
        scratch_shapes=[
            pltpu.VMEM((RING * tr, hw), bf16),
            pltpu.VMEM((RING * tr, hw), bf16),
            pltpu.VMEM((RING, META, LANES), f32),
            pltpu.VMEM((slots, hw), bf16),
            pltpu.VMEM((slots, hw), bf16),
            pltpu.VMEM((slots, hw), bf16),
            pltpu.VMEM((max(9 * META, hid), quarter), bf16),
            pltpu.VMEM((9 * META, quarter), bf16),
            pltpu.VMEM((max(9 * META, hid), quarter), bf16),
            pltpu.VMEM((max(9 * META, hid), quarter), bf16),
            pltpu.VMEM((hw, hid), bf16),
            pltpu.VMEM((hid + LANES, hw), bf16),
            pltpu.VMEM((slots, hid), f32),
            pltpu.VMEM((slots, hid), f32),
            pltpu.VMEM((slots, hid), bf16),
            pltpu.VMEM((slots, hid), bf16),
            pltpu.VMEM((slots, hid), bf16),
            pltpu.VMEM((slots, hid), bf16),
            pltpu.VMEM((COLUMNS * 16, hid), f32),
            pltpu.VMEM((COLUMNS * 16, hid), f32),
            pltpu.VMEM((COLUMNS * 16, LANES), f32),
            pltpu.VMEM((16, hw), f32),
            pltpu.VMEM((8, 2 * LANES), f32),
            pltpu.VMEM((9, 8, 2 * LANES), f32),
            pltpu.VMEM((8, 2 * LANES), f32),
            dma((5,)), dma((5,)),
            dma((12,)), dma((12,)),
        ]
        + [dma((5, 9)) for _ in range(8)]
        + [dma((5, 6)) for _ in range(2)]
        + [
            dma((5,)), dma((5,)),
            dma((5,)), dma((5,)),
            dma((9,)), dma((9,)),
            dma((1,)), dma((1,)),
            dma((2,)), dma((2,)),
        ],
        compiler_params=pltpu.CompilerParams(
            collective_id=0, has_side_effects=True, vmem_limit_bytes=63 * 2**20
        ),
        cost_estimate=pl.CostEstimate(flops=40 * 10**9, bytes_accessed=30 * 10**6, transcendentals=10**6),
        name="routed_step",
    )(tokens, readout, meta, own, w_up[0], w_down[0])
    here = col * 16 + 12 + x
    losses = lax.dynamic_slice(small, (0, here), (1, 1)).reshape(1)
    kl_terms = lax.dynamic_slice(small, (1, here), (1, 1)).reshape(1)
    return up[None], down[None], losses, kl_terms


def solution(mesh):
    return jax.shard_map(
        local,
        mesh=mesh,
        in_specs=(
            P(("dp", "expert"), None),
            P(),
            P(("dp", "expert"), None),
            P("expert", None, None),
            P("expert", None, None),
            P(("dp", "expert"), None),
            P(("dp", "expert")),
            P(("dp", "expert")),
            P(("dp", "expert"), None),
            P(("dp", "expert")),
            P(("dp", "expert")),
        ),
        out_specs=(
            P("expert", "dp", None),
            P("expert", None, "dp"),
            P(("dp", "expert")),
            P(("dp", "expert")),
        ),
        check_vma=False,
    )
```

```python
import functools

import jax
import jax.numpy as jnp
from jax import lax
from jax.experimental import pallas as pl
from jax.experimental.pallas import tpu as pltpu
from jax.sharding import PartitionSpec as P

MESH = pl.DeviceIdType.MESH
routed_scale = 16.0
kto_beta = 0.1
loss_scale = 1024.0
f32, bf16 = jnp.float32, jnp.bfloat16

RING = 4
COLUMNS = 16
LANES = 128
META = 80
PARTS = (32, 32, 16)
PART_AT = (0, 32, 64)
CUTS = ((0, 512), (512, 1024), (1536, 1024))
NT = (((1,), (1,)), ((), ()))
TN = (((0,), (0,)), ((), ()))


def split3(value):
    high = value.astype(bf16).astype(f32)
    middle = (value - high).astype(bf16).astype(f32)
    low = (value - high - middle).astype(bf16).astype(f32)
    return high, middle, low


def place():
    dp, ex = lax.axis_index("dp"), lax.axis_index("expert")
    return dp // 2, dp % 2, ex % 2, ex // 2


def kernel(
    cap, hw, tok, rdo, route, ids, logp, prompt, label, mate, klr, wu_hbm, wd_hbm,
    up_hbm, down_hbm, small_out,
    xb, yb, mb, ob, xin, yin, m1x, m2x, m1y, m2y, wu, wd, pa, ra, pas, pap, ras, rap, prs, hst, wst,
    exty, meta, gsc, acc, arb, arc,
    lsem, osem, ag_s, ag_r, a1s, a1r, a2s, a2r, b1s, b1r, b2s, b2r, ds, dr,
    ps, pr, qs, qr, ar_s, ar_r, c_s, c_r, g_s, g_r,
):
    rb = META
    tr = tok.shape[0]
    hid = wu.shape[1]
    slots = COLUMNS * rb
    x_lo, core, x_hi, col = place()
    dp, ex = lax.axis_index("dp"), lax.axis_index("expert")
    x = x_hi * 2 + x_lo
    y, z = col % RING, col // RING

    def dev_x(xx):
        return ((xx % 2) * 2 + core, col * 2 + xx // 2)

    def dev_col(cc):
        return (dp, cc * 2 + x_hi)

    sibling = (x_lo * 2 + 1 - core, ex)
    partner = ((1 - x_lo) * 2 + core, ex)

    def plus(dz, dy):
        return ((z + dz) % RING) * RING + (y + dy) % RING

    def minus(dz, dy):
        return ((z + RING - dz) % RING) * RING + (y + RING - dy) % RING

    def rows(start, size):
        return pl.ds(pl.multiple_of(start, 16), size)

    def remote(src, dst, ss, rs, dev):
        return pltpu.make_async_remote_copy(
            src_ref=src, dst_ref=dst, send_sem=ss, recv_sem=rs, device_id=dev, device_id_type=MESH
        )

    def loop(count, body, start=0):
        def step(i, carry):
            body(i)
            return carry

        lax.fori_loop(start, count, step, 0)

    barrier = pltpu.get_barrier_semaphore()

    def greet(dev):
        pl.semaphore_signal(barrier, inc=1, device_id=dev, device_id_type=MESH)

    loop(RING, lambda d: greet(dev_x((x + d) % RING)), 1)
    loop(RING, lambda d: greet(dev_col(plus(d, 0))), 1)
    loop(RING, lambda d: greet(dev_col(plus(0, d))), 1)
    greet(sibling)
    half = pl.ds(pl.multiple_of(x_lo * hw, LANES), hw)
    away = pl.ds(pl.multiple_of((1 - x_lo) * hw, LANES), hw)
    mine = pl.ds(pl.multiple_of(x * tr, LANES), tr)
    routes = route.shape[0]
    locals_ = [
        pltpu.make_async_copy(tok.at[:, half], xb.at[mine], lsem.at[0]),
        pltpu.make_async_copy(rdo.at[:, half], yb.at[mine], lsem.at[1]),
        pltpu.make_async_copy(tok.at[:, away], ob.at[pl.ds(0, tr)], lsem.at[2]),
        pltpu.make_async_copy(route.at[:, half], ob.at[pl.ds(2 * tr, routes)], lsem.at[3]),
        pltpu.make_async_copy(route.at[:, away], ob.at[pl.ds(2 * tr + routes, routes)], lsem.at[4]),
        pltpu.make_async_copy(rdo.at[:, away], ob.at[pl.ds(tr, tr)], lsem.at[5]),
        pltpu.make_async_copy(wu_hbm.at[half], wu, lsem.at[6]),
        pltpu.make_async_copy(wd_hbm.at[:, half], wd.at[pl.ds(0, hid)], lsem.at[7]),
    ]
    for copy in locals_:
        copy.start()
    pl.semaphore_wait(barrier, 3 * (RING - 1) + 1)

    pieces = ((0, 0, hw),) + tuple((1, start, size) for start, size in CUTS) + ((2, 0, hw),)

    def ring_copy(which, d):
        to = (x + d) % RING
        kind, start, size = pieces[which]
        cols = pl.ds(pl.multiple_of((to % 2) * hw + start, LANES), size)
        here = pl.ds(start, size)
        src = (meta.at[to], tok.at[:, cols], rdo.at[:, cols])[kind]
        dst = (mb.at[x], xb.at[mine, here], yb.at[mine, here])[kind]
        return remote(src, dst, ag_s.at[which * 3 + d - 1], ag_r.at[which * 3 + d - 1], dev_x(to))

    rings = [[ring_copy(which, d) for d in (1, 3, 2)] for which in range(len(pieces))]

    def start_ring(which):
        for copy in rings[which]:
            copy.start()

    def wait_ring(which):
        for copy in rings[which]:
            copy.wait_recv()

    start_ring(1)
    for copy in locals_:
        copy.wait()

    logits = lax.dot_general(
        ob[pl.ds(2 * tr, routes), :], xb[mine, :], NT, preferred_element_type=f32
    ) + lax.dot_general(
        ob[pl.ds(2 * tr + routes, routes), :], ob[pl.ds(0, tr), :], NT, preferred_element_type=f32
    )
    scores = jnp.exp(logits)
    experts = 2 * COLUMNS
    gsc[...] = routed_scale * scores[:experts] / jnp.sum(scores, axis=0, keepdims=True)
    spread = lax.broadcasted_iota(jnp.int32, (experts, tr), 0)
    spread = (spread % COLUMNS) * 2 + spread // COLUMNS
    hits = jnp.zeros((experts, tr), f32)
    for k in range(ids.shape[0]):
        hits = hits + jnp.where(ids[k : k + 1, :] == spread, 1.0, 0.0)
    ahead = lax.broadcasted_iota(jnp.int32, (tr, tr), 0) < lax.broadcasted_iota(jnp.int32, (tr, tr), 1)
    rank = jnp.dot(hits.astype(bf16), jnp.where(ahead, 1.0, 0.0).astype(bf16), preferred_element_type=f32)
    want = jnp.where((hits > 0.5) & (rank < cap), rank + (cap * x).astype(f32), -1.0)
    ones = jnp.ones((16, tr), bf16)
    base_here = jnp.dot(ones, xb[mine, :], preferred_element_type=f32)[0:1]
    base_away = jnp.dot(ones, ob[pl.ds(0, tr), :], preferred_element_type=f32)[0:1]
    words = prompt[...].astype(f32)
    lanes = lax.broadcasted_iota(jnp.int32, (1, 2 * LANES), 1)
    spot = lanes == col * 16 + 12 + x
    pair = ((mate[0] // 2) * 16 + (mate[0] % 2) * 2 + x_lo).astype(f32)
    pair = jnp.where(spot, pair, 0.0)
    for lo in range(2):
        base = jnp.where(x_lo == lo, base_here, base_away)
        for hi in range(2):
            xx = 2 * hi + lo
            meta[xx, 0:16] = want[16 * hi : 16 * hi + 16]
            meta[xx, 16:32] = gsc[pl.ds(hi, 16, stride=2), :]
            for j in range(hw // LANES):
                meta[xx, 32 + j : 33 + j] = words[:, lo * hw + j * LANES : lo * hw + (j + 1) * LANES]
                meta[xx, 52 + j : 53 + j] = base[:, j * LANES : (j + 1) * LANES]
            meta[xx, 72:80] = jnp.zeros((8, LANES), f32)
            meta[xx, 72:73] = pair[:, :LANES]
            meta[xx, 73:74] = pair[:, LANES:]
    start_ring(0)
    mb[x] = meta[x]
    margin = -jnp.sum(logp[...], axis=1, keepdims=True)
    for j in range(hw // 512):
        lane = pl.ds(j * 512, 512)
        both = xb[mine, lane].astype(f32) * yb[mine, lane].astype(f32)
        both += ob[pl.ds(0, tr), lane].astype(f32) * ob[pl.ds(tr, tr), lane].astype(f32)
        margin += jnp.sum(jnp.sum(both, axis=0, keepdims=True), axis=1, keepdims=True)
    acc[...] = jnp.zeros_like(acc)
    acc[0:1, :] = jnp.where(spot, -klr[0], 0.0)
    acc[1:2, :] = jnp.where(spot, margin, 0.0)
    acc[2:3, :] = jnp.where(spot, jnp.where(label[0] == 1, 1.0, -1.0), 0.0)
    wait_ring(0)

    exty[...] = jnp.zeros_like(exty)
    tall = lax.broadcasted_iota(jnp.int32, (LANES, LANES), 0)
    for j in range(hw // LANES):
        lane = pl.ds(j * LANES, LANES)
        for b in range(RING):
            exty[12 + b : 13 + b, lane] = mb[b, 32 + j : 33 + j, :]
        terms = split3(mb[x, 52 + j : 53 + j, :]) + split3(mb[x + 1 - 2 * x_lo, 52 + j : 53 + j, :])
        block = jnp.zeros((LANES, LANES), f32)
        for i, term in enumerate(terms):
            block = jnp.where(tall == i, term, block)
        wd[pl.ds(hid, LANES), lane] = block.astype(bf16)

    def shipment(n):
        if n < 3:
            start, width = CUTS[n]
            return rb, 0, start, width, 0, start // 2, m1x, m2x, xin
        size, at = PARTS[n - 3], PART_AT[n - 3]
        return size, at * COLUMNS, 0, hw, at * 9, 0, m1y, m2y, yin

    def block(n, cc):
        size, base = shipment(n)[:2]
        return rows(base + cc * size, size)

    def halves(n):
        start, width = shipment(n)[2:4]
        return pl.ds(start, width // 2), pl.ds(start + width // 2, width // 2), pl.ds(start, width)

    def held(n, i):
        size, _, _, width, base, at = shipment(n)[:6]
        return rows(base + i * size, size), pl.ds(at, width // 2)

    def turn(i):
        return 1 + i // 3, 1 + i % 3

    def a_first(n, i):
        dz, dy = turn(i)
        there = held(n, i)
        return remote(
            ob.at[block(n, plus(dz, dy)), halves(n)[0]], shipment(n)[6].at[there[0], there[1]],
            a1s.at[n, i], a1r.at[n, i], dev_col(plus(0, dy)),
        )

    def a_second(n, i):
        dz, dy = turn(i)
        there = held(n, i)
        return remote(
            shipment(n)[6].at[there[0], there[1]], shipment(n)[8].at[block(n, minus(0, dy)), halves(n)[0]],
            a2s.at[n, i], a2r.at[n, i], dev_col(plus(dz, 0)),
        )

    def b_first(n, i):
        dz, dy = turn(i)
        there = held(n, i)
        return remote(
            ob.at[block(n, plus(dz, dy)), halves(n)[1]], shipment(n)[7].at[there[0], there[1]],
            b1s.at[n, i], b1r.at[n, i], dev_col(plus(dz, 0)),
        )

    def b_second(n, i):
        dz, dy = turn(i)
        there = held(n, i)
        return remote(
            shipment(n)[7].at[there[0], there[1]], shipment(n)[8].at[block(n, minus(dz, 0)), halves(n)[1]],
            b2s.at[n, i], b2r.at[n, i], dev_col(plus(0, dy)),
        )

    def straight(n, i):
        dz, dy = (i + 1) * (1 - i // 3), (i - 2) * (i // 3)
        to = plus(dz, dy)
        return remote(
            ob.at[block(n, to), halves(n)[2]], shipment(n)[8].at[block(n, col), halves(n)[2]],
            ds.at[n, i], dr.at[n, i], dev_col(to),
        )

    def keep(n):
        cols = halves(n)[2]
        return pltpu.make_async_copy(ob.at[block(n, col), cols], shipment(n)[8].at[block(n, col), cols], osem.at[n])

    wide = 512

    def picks(cc, start, size):
        want = jnp.concatenate([mb[b, pl.ds(cc, 1), :] for b in range(RING)], axis=1)
        row = start + lax.broadcasted_iota(jnp.int32, (size, RING * tr), 0).astype(f32)
        return jnp.where(row == want, 1.0, 0.0).astype(bf16)

    def gate_rows(cc):
        gate = jnp.concatenate([mb[b, pl.ds(16 + cc, 1), :] for b in range(RING)], axis=1)
        row = lax.broadcasted_iota(jnp.int32, (16, RING * tr), 0)
        lifted = jnp.zeros((16, RING * tr), f32)
        for i, term in enumerate(split3(gate)):
            lifted = jnp.where(row == 12 + i, term, lifted)
        gates = lax.dot_general(lifted.astype(bf16), picks(cc, 0, LANES), NT, preferred_element_type=f32)
        pair = [sum(mb[b, 72 + i : 73 + i, :] for b in range(RING)) for i in range(2)]
        pair = jnp.concatenate(pair, axis=1)
        gates = jnp.concatenate([gates, jnp.zeros((16, LANES), f32)], axis=1)
        last = lax.broadcasted_iota(jnp.int32, (16, 2 * LANES), 0) == 15
        return gates + jnp.where(last, pair, 0.0)

    def build(n):
        size, base, start, width = shipment(n)[:4]
        at = 0 if n < 3 else PART_AT[n - 3]
        source = xb if n < 3 else yb

        def plane(zz):
            pick = jnp.concatenate([picks(zz * RING + i, at, size) for i in range(RING)], axis=0)
            place_ = rows(base + zz * (RING * size), RING * size)
            for lo in range(start, start + width, wide):
                lane = pl.ds(lo, min(wide, start + width - lo))
                made = jnp.dot(pick, source[:, lane], preferred_element_type=f32)
                if n == 5:
                    made = made + jnp.concatenate([exty[:, lane]] * RING, axis=0)
                ob[place_, lane] = made.astype(bf16)
            if n == 0:
                for i in range(RING):
                    tail = rows(zz * (RING * size) + i * size + 64, 16)
                    first = pl.ds(0, 2 * LANES)
                    ob[tail, first] = (ob[tail, first].astype(f32) + gate_rows(zz * RING + i)).astype(bf16)

        def go(k):
            dz = (k + 1) % RING
            plane((z + dz) % RING)

            @pl.when(dz > 0)
            def _():
                for dy in range(1, RING):
                    i = (dz - 1) * 3 + dy - 1
                    a_first(n, i).start()
                    b_first(n, i).start()
                straight(n, dz - 1).start()

            @pl.when(dz == 0)
            def _():
                for dy in range(1, RING):
                    straight(n, 2 + dy).start()
                keep(n).start()

        loop(RING, go)

    def forward(n):
        def go(i):
            a_first(n, i).wait_recv()
            a_second(n, i).start()
            b_first(n, i).wait_recv()
            b_second(n, i).start()

        loop(9, go)

    def built_sent(n):
        def go(i):
            a_first(n, i).wait_send()
            b_first(n, i).wait_send()

        loop(9, go)
        loop(6, lambda i: straight(n, i).wait_send())
        if n < 3:
            keep(n).wait()

    def forwards_sent(n):
        def go(i):
            a_second(n, i).wait_send()
            b_second(n, i).wait_send()

        loop(9, go)

    def arrived(n):
        def go(i):
            a_second(n, i).wait_recv()
            b_second(n, i).wait_recv()

        loop(9, go)
        loop(6, lambda i: straight(n, i).wait_recv())
        if n >= 3:
            keep(n).wait()

    span = 256

    def pair_x(j):
        at = rows(j * span, span)
        return remote(pas.at[at], pap.at[at], ps.at[j], pr.at[j], partner)

    def pair_y(j):
        at = rows(j * span, span)
        return remote(ras.at[at], rap.at[at], qs.at[j], qr.at[j], partner)

    def use_x(j):
        at = rows(j * span, span)
        part = jnp.dot(xin[at, :], wu[...], preferred_element_type=f32)
        pa[at, :] = part
        pas[at, :] = part.astype(bf16)
        pair_x(j).start()

    def use_y(j):
        at = rows(j * span, span)
        part = lax.dot_general(yin[at, :], wd[pl.ds(0, hid), :], NT, preferred_element_type=f32)
        ra[at, :] = part
        ras[at, :] = part.astype(bf16)
        pair_y(j).start()

    def meet(p):
        size, at = PARTS[p], PART_AT[p]
        shape = (size, 2 * LANES)
        lane = lax.broadcasted_iota(jnp.int32, shape, 1)
        row = at + lax.broadcasted_iota(jnp.int32, shape, 0)
        row_lane = jnp.where(row < RING * cap, 12 + row // cap, -1)
        square = at + lax.broadcasted_iota(jnp.int32, (size, LANES), 0) == lax.broadcasted_iota(
            jnp.int32, (size, LANES), 1
        )
        first = lax.broadcasted_iota(jnp.int32, (16, size), 0)
        which = (at + lax.broadcasted_iota(jnp.int32, (16, size), 1)) // cap
        gather = jnp.where(first == which, 1.0, 0.0).astype(bf16)

        def go(cc):
            xr_ = rows(cc * rb + at, size)
            yr_ = rows(at * COLUMNS + cc * size, size)
            tail = xin[rows(cc * rb + 64, 16), pl.ds(0, 2 * LANES)].astype(f32)
            p_ = pa[xr_, :] + pap[xr_, :].astype(f32)
            r = ra[yr_, :] + rap[yr_, :].astype(f32)
            gate = jnp.sum(tail[12:15, :LANES], axis=0, keepdims=True)
            gate = jnp.sum(jnp.where(square, gate, 0.0), axis=1, keepdims=True)
            logistic = jax.nn.sigmoid(p_)
            gated = gate * (p_ * logistic)
            ra[yr_, :] = gated
            pa[xr_, :] = gate * r * (logistic * (1.0 + p_ * (1.0 - logistic)))
            margin = jnp.sum(gated * r, axis=1, keepdims=True)
            hot = jnp.where(lane - cc * 16 == row_lane, 1.0, 0.0)
            acc[1:2, :] += 0.5 * jnp.sum(hot * margin, axis=0, keepdims=True)
            spot = rows(cc * 16, 16)
            summed = jnp.dot(gather, gated.astype(bf16), preferred_element_type=f32)
            if p == 0:
                acc[3:4, :] += tail[15:16]
                hst[spot, :] = summed
            else:
                hst[spot, :] += summed
            if p == 2:
                prs[spot, :] = r

        loop(COLUMNS, go)

    wait_ring(1)
    start_ring(2)
    build(0)
    wait_ring(2)
    start_ring(3)
    build(1)
    forward(0)
    wait_ring(3)
    start_ring(4)
    build(2)
    forward(1)
    built_sent(0)
    built_sent(1)
    forward(2)
    built_sent(2)
    wait_ring(4)
    build(3)
    build(4)
    for n in range(3):
        arrived(n)
    loop(2, use_x)
    forward(3)
    loop(5, use_x, 2)
    build(5)
    forward(4)
    arrived(3)
    loop(2, use_y)
    forward(5)
    arrived(4)
    loop(4, use_y, 2)
    loop(5, lambda j: pair_x(j).wait_recv())
    loop(2, lambda j: pair_y(j).wait_recv())
    meet(0)
    arrived(5)
    last_at = rows(4 * span, span)
    last_part = lax.dot_general(yin[last_at, :], wd[...], NT, preferred_element_type=f32)
    ra[last_at, :] = last_part[:, :hid]
    ras[last_at, :] = last_part[:, :hid].astype(bf16)
    pair_y(4).start()
    wst[...] = last_part[:, hid:]
    loop(4, lambda j: pair_y(j).wait_recv(), 2)
    meet(1)
    pair_y(4).wait_recv()
    meet(2)

    wide_t = wst[...].T
    base_own = wide_t[0:1] + wide_t[1:2] + wide_t[2:3]
    base_other = wide_t[3:4] + wide_t[4:5] + wide_t[5:6]
    pairs = acc[3:4, :]
    terms = 0.5 * lax.dot_general(
        hst[...], prs[...], NT, precision=lax.Precision.HIGHEST, preferred_element_type=f32
    )
    named = lax.broadcasted_iota(jnp.int32, terms.shape, 0)
    terms += jnp.where(named == col * 16 + x, base_own, 0.0)
    terms += jnp.where(named == col * 16 + x + 1 - 2 * x_lo, base_other, 0.0)
    used = lax.broadcasted_iota(jnp.int32, (1, 2 * LANES), 1) % 16 >= 12
    chosen = jnp.where((named.astype(f32) == pairs) & used, terms, 0.0)
    acc[0:1, :] += jnp.sum(chosen, axis=0, keepdims=True)

    def ring_sum(axis, dev):
        copies = [
            remote(acc, arb.at[axis * 3 + d - 1], ar_s.at[axis * 3 + d - 1], ar_r.at[axis * 3 + d - 1], dev(d))
            for d in (1, 3, 2)
        ]
        for copy in copies:
            copy.start()
        for copy in copies:
            copy.wait()
        acc[...] = acc[...] + arb[axis * 3] + arb[axis * 3 + 1] + arb[axis * 3 + 2]

    ring_sum(0, lambda d: dev_x((x + d) % RING))
    ring_sum(1, lambda d: dev_col(plus(0, d)))
    ring_sum(2, lambda d: dev_col(plus(d, 0)))
    for n in range(3, 6):
        built_sent(n)
    for n in range(6):
        forwards_sent(n)
    loop(5, lambda j: pair_x(j).wait_send())
    loop(5, lambda j: pair_y(j).wait_send())
    for ring in rings:
        for copy in ring:
            copy.wait_send()
    swap = remote(acc, arc, c_s.at[0], c_r.at[0], sibling)
    swap.start()
    swap.wait()
    kl_row = jnp.where(used, acc[0:1, :], 0.0)
    kl_other = jnp.where(used, arc[0:1, :], 0.0)
    count = RING * COLUMNS * 2
    anchor = jnp.sum(kl_row + kl_other, axis=1, keepdims=True) / count
    signed = acc[2:3, :]
    kept = jax.nn.sigmoid(kto_beta * signed * (acc[1:2, :] - anchor))
    slope = -loss_scale * kto_beta * signed * kept * (1.0 - kept)
    small_out[...] = jnp.zeros_like(small_out)
    small_out[0:1, :] = 1.0 - kept
    small_out[1:2, :] = kl_row

    def scaled(source, dst, start, size, at):
        lane = lax.broadcasted_iota(jnp.int32, (size, 2 * LANES), 1)
        row = at + lax.broadcasted_iota(jnp.int32, (size, 2 * LANES), 0)
        row_lane = jnp.where(row < RING * cap, 12 + row // cap, -1)

        def go(cc):
            here = rows(start + cc * size, size)
            factor = jnp.sum(jnp.where(lane - cc * 16 == row_lane, slope, 0.0), axis=1, keepdims=True)
            dst[here, :] = (source[here, :] * factor).astype(bf16)

        loop(COLUMNS, go)

    quarter = hw // 2
    step = 640
    other = (1 - core) * quarter
    this = core * quarter
    hid_t = m2y.at[pl.ds(0, hid)]
    up_got, down_got = rap, m1y.at[pl.ds(0, hid)]
    up_out, down_out = pl.ds(0, hid), m1x.at[pl.ds(0, hid)]
    down_sent = pl.ds(quarter, quarter)

    def up_block(start, j):
        at = pl.ds(pl.multiple_of(start + j * step, LANES), step)
        return lax.dot_general(xin[:, at], pas[...], TN, preferred_element_type=f32)

    def down_block(start, j):
        at = pl.ds(pl.multiple_of(start + j * step, LANES), step)
        return jnp.dot(hid_t[...], yin[:, at], preferred_element_type=f32)

    def piece(j, base=0):
        return pl.ds(pl.multiple_of(base + j * step, LANES), step)

    def other_up(j):
        pap[piece(j), :] = up_block(other, j).astype(bf16)

    def other_down(j):
        ob[pl.ds(0, hid), piece(j, quarter)] = down_block(other, j).astype(bf16)

    def this_up(j):
        ob[piece(j), up_out] = (up_block(this, j) + up_got[piece(j), :].astype(f32)).astype(bf16)

    def this_down(j):
        down_out[:, piece(j)] = (down_block(this, j) + down_got[:, piece(j)].astype(f32)).astype(bf16)

    up_copy = remote(pap, up_got, g_s.at[0], g_r.at[0], sibling)
    down_copy = remote(ob.at[pl.ds(0, hid), down_sent], down_got, g_s.at[1], g_r.at[1], sibling)
    blocks = quarter // step
    scaled(pa, pas, 0, rb, 0)
    loop(blocks, other_up)
    up_copy.start()
    for p in range(3):
        scaled(ra, ras, PART_AT[p] * COLUMNS, PARTS[p], PART_AT[p])
    for j in range(slots // span):
        at = pl.ds(j * span, span)
        hid_t[:, at] = ras[at, :].T
    loop(blocks, other_down)
    down_copy.start()
    up_copy.wait_recv()
    loop(blocks, this_up)
    up_done = pltpu.make_async_copy(ob.at[pl.ds(0, quarter), up_out], up_hbm, lsem.at[0])
    up_done.start()
    down_copy.wait_recv()
    loop(blocks, this_down)
    down_done = pltpu.make_async_copy(down_out, down_hbm, lsem.at[1])
    down_done.start()
    up_copy.wait_send()
    down_copy.wait_send()
    up_done.wait()
    down_done.wait()


def local(
    tokens, router, expert_ids, w_up, w_down, readout, ref_logp, labels, prompt_read, kl_pair, kl_ref
):
    experts = lax.axis_size("expert")
    tr, width = tokens.shape
    top = expert_ids.shape[1]
    cap = 4 * tr * top // (5 * experts)
    hid = w_up.shape[2]
    hw = width // 2
    x_lo, core, x_hi, col = place()
    x = x_hi * 2 + x_lo

    slots = COLUMNS * META
    quarter = hw // 2
    dma = pltpu.SemaphoreType.DMA
    any_ = pl.BlockSpec(memory_space=pl.ANY)
    vmem = pl.BlockSpec(memory_space=pltpu.VMEM)
    smem = pl.BlockSpec(memory_space=pltpu.SMEM)
    up, down, small = pl.pallas_call(
        functools.partial(kernel, cap, hw),
        out_shape=(
            jax.ShapeDtypeStruct((quarter, hid), bf16),
            jax.ShapeDtypeStruct((hid, quarter), bf16),
            jax.ShapeDtypeStruct((8, 2 * LANES), f32),
        ),
        in_specs=[any_, any_, any_, vmem, vmem, vmem, smem, smem, smem, any_, any_],
        out_specs=(any_, any_, vmem),
        scratch_shapes=[
            pltpu.VMEM((RING * tr, hw), bf16),
            pltpu.VMEM((RING * tr, hw), bf16),
            pltpu.VMEM((RING, META, LANES), f32),
            pltpu.VMEM((slots, hw), bf16),
            pltpu.VMEM((slots, hw), bf16),
            pltpu.VMEM((slots, hw), bf16),
            pltpu.VMEM((max(9 * META, hid), quarter), bf16),
            pltpu.VMEM((9 * META, quarter), bf16),
            pltpu.VMEM((max(9 * META, hid), quarter), bf16),
            pltpu.VMEM((max(9 * META, hid), quarter), bf16),
            pltpu.VMEM((hw, hid), bf16),
            pltpu.VMEM((hid + LANES, hw), bf16),
            pltpu.VMEM((slots, hid), f32),
            pltpu.VMEM((slots, hid), f32),
            pltpu.VMEM((slots, hid), bf16),
            pltpu.VMEM((slots, hid), bf16),
            pltpu.VMEM((slots, hid), bf16),
            pltpu.VMEM((slots, hid), bf16),
            pltpu.VMEM((COLUMNS * 16, hid), f32),
            pltpu.VMEM((COLUMNS * 16, hid), f32),
            pltpu.VMEM((COLUMNS * 16, LANES), f32),
            pltpu.VMEM((16, hw), f32),
            pltpu.VMEM((RING, META, LANES), f32),
            pltpu.VMEM((2 * COLUMNS, tr), f32),
            pltpu.VMEM((8, 2 * LANES), f32),
            pltpu.VMEM((9, 8, 2 * LANES), f32),
            pltpu.VMEM((8, 2 * LANES), f32),
            dma((8,)), dma((6,)),
            dma((15,)), dma((15,)),
        ]
        + [dma((6, 9)) for _ in range(8)]
        + [dma((6, 6)) for _ in range(2)]
        + [
            dma((5,)), dma((5,)),
            dma((5,)), dma((5,)),
            dma((9,)), dma((9,)),
            dma((1,)), dma((1,)),
            dma((2,)), dma((2,)),
        ],
        compiler_params=pltpu.CompilerParams(
            collective_id=0, has_side_effects=True, vmem_limit_bytes=63 * 2**20
        ),
        cost_estimate=pl.CostEstimate(flops=40 * 10**9, bytes_accessed=30 * 10**6, transcendentals=10**6),
        name="routed_step",
    )(
        tokens, readout, router.T, expert_ids.T, ref_logp.reshape(1, tr), prompt_read, labels, kl_pair, kl_ref,
        w_up[0], w_down[0],
    )
    here = col * 16 + 12 + x
    losses = lax.dynamic_slice(small, (0, here), (1, 1)).reshape(1)
    kl_terms = lax.dynamic_slice(small, (1, here), (1, 1)).reshape(1)
    return up[None], down[None], losses, kl_terms


def solution(mesh):
    return jax.shard_map(
        local,
        mesh=mesh,
        in_specs=(
            P(("dp", "expert"), None),
            P(),
            P(("dp", "expert"), None),
            P("expert", None, None),
            P("expert", None, None),
            P(("dp", "expert"), None),
            P(("dp", "expert")),
            P(("dp", "expert")),
            P(("dp", "expert"), None),
            P(("dp", "expert")),
            P(("dp", "expert")),
        ),
        out_specs=(
            P("expert", "dp", None),
            P("expert", None, "dp"),
            P(("dp", "expert")),
            P(("dp", "expert")),
        ),
        check_vma=False,
    )
```

```python
import functools

import jax
import jax.numpy as jnp
from jax import lax
from jax.experimental import pallas as pl
from jax.experimental.pallas import tpu as pltpu
from jax.sharding import PartitionSpec as P

MESH = pl.DeviceIdType.MESH
routed_scale = 16.0
kto_beta = 0.1
loss_scale = 1024.0
f32, bf16 = jnp.float32, jnp.bfloat16

RING = 4
COLUMNS = 16
LANES = 128
META = 80
PARTS = (32, 32, 16)
PART_AT = (0, 32, 64)
CUTS = ((0, 512), (512, 1024), (1536, 1024))
NT = (((1,), (1,)), ((), ()))
TN = (((0,), (0,)), ((), ()))


def split3(value):
    high = value.astype(bf16).astype(f32)
    middle = (value - high).astype(bf16).astype(f32)
    low = (value - high - middle).astype(bf16).astype(f32)
    return high, middle, low


def place():
    dp, ex = lax.axis_index("dp"), lax.axis_index("expert")
    return dp // 2, dp % 2, ex % 2, ex // 2


def kernel(
    cap, hw, tok, rdo, route, ids, logp, prompt, label, mate, klr, wu_hbm, wd_hbm,
    up_hbm, down_hbm, small_out,
    xb, yb, mb, ob, xin, yin, m1x, m2x, m1y, m2y, wu, wd, pa, ra, pas, pap, ras, rap, prs, hst, wst,
    exty, meta, gsc, acc, arb, arc,
    lsem, osem, ag_s, ag_r, a1s, a1r, a2s, a2r, b1s, b1r, b2s, b2r, ds, dr,
    ps, pr, qs, qr, ar_s, ar_r, g_s, g_r,
):
    rb = META
    tr = tok.shape[0]
    hid = wu.shape[1]
    slots = COLUMNS * rb
    x_lo, core, x_hi, col = place()
    dp, ex = lax.axis_index("dp"), lax.axis_index("expert")
    x = x_hi * 2 + x_lo
    y, z = col % RING, col // RING

    def dev_x(xx):
        return ((xx % 2) * 2 + core, col * 2 + xx // 2)

    def dev_across(xx):
        return ((xx % 2) * 2 + 1 - core, col * 2 + xx // 2)

    def dev_col(cc):
        return (dp, cc * 2 + x_hi)

    sibling = (x_lo * 2 + 1 - core, ex)
    partner = ((1 - x_lo) * 2 + core, ex)

    def plus(dz, dy):
        return ((z + dz) % RING) * RING + (y + dy) % RING

    def minus(dz, dy):
        return ((z + RING - dz) % RING) * RING + (y + RING - dy) % RING

    def rows(start, size):
        return pl.ds(pl.multiple_of(start, 16), size)

    def remote(src, dst, ss, rs, dev):
        return pltpu.make_async_remote_copy(
            src_ref=src, dst_ref=dst, send_sem=ss, recv_sem=rs, device_id=dev, device_id_type=MESH
        )

    def loop(count, body, start=0):
        def step(i, carry):
            body(i)
            return carry

        lax.fori_loop(start, count, step, 0)

    barrier = pltpu.get_barrier_semaphore()

    def greet(dev):
        pl.semaphore_signal(barrier, inc=1, device_id=dev, device_id_type=MESH)

    loop(RING, lambda d: greet(dev_x((x + d) % RING)), 1)
    loop(RING, lambda d: greet(dev_across((x + d) % RING)))
    loop(COLUMNS, lambda k: greet(dev_col(plus(k // RING, k % RING))), 1)
    half = pl.ds(pl.multiple_of(x_lo * hw, LANES), hw)
    away = pl.ds(pl.multiple_of((1 - x_lo) * hw, LANES), hw)
    mine = pl.ds(pl.multiple_of(x * tr, LANES), tr)
    routes = route.shape[0]
    locals_ = [
        pltpu.make_async_copy(tok.at[:, half], xb.at[mine], lsem.at[0]),
        pltpu.make_async_copy(rdo.at[:, half], yb.at[mine], lsem.at[1]),
        pltpu.make_async_copy(tok.at[:, away], ob.at[pl.ds(0, tr)], lsem.at[2]),
        pltpu.make_async_copy(route.at[:, half], ob.at[pl.ds(2 * tr, routes)], lsem.at[3]),
        pltpu.make_async_copy(route.at[:, away], ob.at[pl.ds(2 * tr + routes, routes)], lsem.at[4]),
        pltpu.make_async_copy(rdo.at[:, away], ob.at[pl.ds(tr, tr)], lsem.at[5]),
        pltpu.make_async_copy(wu_hbm.at[half], wu, lsem.at[6]),
        pltpu.make_async_copy(wd_hbm.at[:, half], wd.at[pl.ds(0, hid)], lsem.at[7]),
    ]
    for copy in locals_:
        copy.start()
    pl.semaphore_wait(barrier, 2 * RING - 1 + COLUMNS - 1)

    pieces = ((0, 0, hw),) + tuple((1, start, size) for start, size in CUTS) + ((2, 0, hw),)

    def ring_copy(which, d):
        to = (x + d) % RING
        kind, start, size = pieces[which]
        cols = pl.ds(pl.multiple_of((to % 2) * hw + start, LANES), size)
        here = pl.ds(start, size)
        src = (meta.at[to], tok.at[:, cols], rdo.at[:, cols])[kind]
        dst = (mb.at[x], xb.at[mine, here], yb.at[mine, here])[kind]
        return remote(src, dst, ag_s.at[which * 3 + d - 1], ag_r.at[which * 3 + d - 1], dev_x(to))

    rings = [[ring_copy(which, d) for d in (1, 3, 2)] for which in range(len(pieces))]

    def start_ring(which):
        for copy in rings[which]:
            copy.start()

    def wait_ring(which):
        for copy in rings[which]:
            copy.wait_recv()

    start_ring(1)
    for copy in locals_[:6]:
        copy.wait()

    logits = lax.dot_general(
        ob[pl.ds(2 * tr, routes), :], xb[mine, :], NT, preferred_element_type=f32
    ) + lax.dot_general(
        ob[pl.ds(2 * tr + routes, routes), :], ob[pl.ds(0, tr), :], NT, preferred_element_type=f32
    )
    scores = jnp.exp(logits)
    experts = 2 * COLUMNS
    gsc[...] = routed_scale * scores[:experts] / jnp.sum(scores, axis=0, keepdims=True)
    spread = lax.broadcasted_iota(jnp.int32, (experts, tr), 0)
    spread = (spread % COLUMNS) * 2 + spread // COLUMNS
    hits = jnp.zeros((experts, tr), f32)
    for k in range(ids.shape[0]):
        hits = hits + jnp.where(ids[k : k + 1, :] == spread, 1.0, 0.0)
    ahead = lax.broadcasted_iota(jnp.int32, (tr, tr), 0) < lax.broadcasted_iota(jnp.int32, (tr, tr), 1)
    rank = jnp.dot(hits.astype(bf16), jnp.where(ahead, 1.0, 0.0).astype(bf16), preferred_element_type=f32)
    want = jnp.where((hits > 0.5) & (rank < cap), rank + (cap * x).astype(f32), -1.0)

    def column_sums(ref, at):
        parts = [ref[at, pl.ds(j * 512, 512)].astype(f32) for j in range(hw // 512)]
        return jnp.concatenate([jnp.sum(part, axis=0, keepdims=True) for part in parts], axis=1)

    base_here = column_sums(xb, mine)
    base_away = column_sums(ob, pl.ds(0, tr))
    words = prompt[...].astype(f32)
    lanes = lax.broadcasted_iota(jnp.int32, (1, 2 * LANES), 1)
    spot = lanes == col * 16 + 12 + x
    pair = ((mate[0] // 2) * 16 + (mate[0] % 2) * 2 + x_lo).astype(f32)
    pair = jnp.where(spot, pair, 0.0)
    for lo in range(2):
        base = jnp.where(x_lo == lo, base_here, base_away)
        for hi in range(2):
            xx = 2 * hi + lo
            meta[xx, 0:16] = want[16 * hi : 16 * hi + 16]
            meta[xx, 16:32] = gsc[pl.ds(hi, 16, stride=2), :]
            for j in range(hw // LANES):
                meta[xx, 32 + j : 33 + j] = words[:, lo * hw + j * LANES : lo * hw + (j + 1) * LANES]
                meta[xx, 52 + j : 53 + j] = base[:, j * LANES : (j + 1) * LANES]
            meta[xx, 72:80] = jnp.zeros((8, LANES), f32)
            meta[xx, 72:73] = pair[:, :LANES]
            meta[xx, 73:74] = pair[:, LANES:]
    start_ring(0)
    mb[x] = meta[x]
    margin = -jnp.sum(logp[...], axis=1, keepdims=True)
    for j in range(hw // 512):
        lane = pl.ds(j * 512, 512)
        both = xb[mine, lane].astype(f32) * yb[mine, lane].astype(f32)
        both += ob[pl.ds(0, tr), lane].astype(f32) * ob[pl.ds(tr, tr), lane].astype(f32)
        margin += jnp.sum(jnp.sum(both, axis=0, keepdims=True), axis=1, keepdims=True)
    acc[...] = jnp.zeros_like(acc)
    acc[0:1, :] = jnp.where(spot, -klr[0], 0.0)
    acc[1:2, :] = jnp.where(spot, margin, 0.0)
    acc[2:3, :] = jnp.where(spot, jnp.where(label[0] == 1, 1.0, -1.0), 0.0)
    wait_ring(0)

    def shipment(n):
        if n < 3:
            start, width = CUTS[n]
            return rb, 0, start, width, 0, start // 2, m1x, m2x, xin
        size, at = PARTS[n - 3], PART_AT[n - 3]
        return size, at * COLUMNS, 0, hw, at * 9, 0, m1y, m2y, yin

    def block(n, cc):
        size, base = shipment(n)[:2]
        return rows(base + cc * size, size)

    def halves(n):
        start, width = shipment(n)[2:4]
        return pl.ds(start, width // 2), pl.ds(start + width // 2, width // 2), pl.ds(start, width)

    def held(n, i):
        size, _, _, width, base, at = shipment(n)[:6]
        return rows(base + i * size, size), pl.ds(at, width // 2)

    def turn(i):
        return 1 + i // 3, 1 + i % 3

    def a_first(n, i):
        dz, dy = turn(i)
        there = held(n, i)
        return remote(
            ob.at[block(n, plus(dz, dy)), halves(n)[0]], shipment(n)[6].at[there[0], there[1]],
            a1s.at[n, i], a1r.at[n, i], dev_col(plus(0, dy)),
        )

    def a_second(n, i):
        dz, dy = turn(i)
        there = held(n, i)
        return remote(
            shipment(n)[6].at[there[0], there[1]], shipment(n)[8].at[block(n, minus(0, dy)), halves(n)[0]],
            a2s.at[n, i], a2r.at[n, i], dev_col(plus(dz, 0)),
        )

    def b_first(n, i):
        dz, dy = turn(i)
        there = held(n, i)
        return remote(
            ob.at[block(n, plus(dz, dy)), halves(n)[1]], shipment(n)[7].at[there[0], there[1]],
            b1s.at[n, i], b1r.at[n, i], dev_col(plus(dz, 0)),
        )

    def b_second(n, i):
        dz, dy = turn(i)
        there = held(n, i)
        return remote(
            shipment(n)[7].at[there[0], there[1]], shipment(n)[8].at[block(n, minus(dz, 0)), halves(n)[1]],
            b2s.at[n, i], b2r.at[n, i], dev_col(plus(0, dy)),
        )

    def straight(n, i):
        dz, dy = (i + 1) * (1 - i // 3), (i - 2) * (i // 3)
        to = plus(dz, dy)
        return remote(
            ob.at[block(n, to), halves(n)[2]], shipment(n)[8].at[block(n, col), halves(n)[2]],
            ds.at[n, i], dr.at[n, i], dev_col(to),
        )

    def keep(n):
        cols = halves(n)[2]
        return pltpu.make_async_copy(ob.at[block(n, col), cols], shipment(n)[8].at[block(n, col), cols], osem.at[n])

    wide = 512

    def picks(cc, start, size):
        want = jnp.concatenate([mb[b, pl.ds(cc, 1), :] for b in range(RING)], axis=1)
        row = start + lax.broadcasted_iota(jnp.int32, (size, RING * tr), 0).astype(f32)
        return jnp.where(row == want, 1.0, 0.0).astype(bf16)

    def gate_rows(cc):
        gate = jnp.concatenate([mb[b, pl.ds(16 + cc, 1), :] for b in range(RING)], axis=1)
        row = lax.broadcasted_iota(jnp.int32, (16, RING * tr), 0)
        lifted = jnp.zeros((16, RING * tr), f32)
        for i, term in enumerate(split3(gate)):
            lifted = jnp.where(row == 12 + i, term, lifted)
        gates = lax.dot_general(lifted.astype(bf16), picks(cc, 0, LANES), NT, preferred_element_type=f32)
        pair = [sum(mb[b, 72 + i : 73 + i, :] for b in range(RING)) for i in range(2)]
        pair = jnp.concatenate(pair, axis=1)
        gates = jnp.concatenate([gates, jnp.zeros((16, LANES), f32)], axis=1)
        last = lax.broadcasted_iota(jnp.int32, (16, 2 * LANES), 0) == 15
        return gates + jnp.where(last, pair, 0.0)

    def build(n):
        size, base, start, width = shipment(n)[:4]
        at = 0 if n < 3 else PART_AT[n - 3]
        source = xb if n < 3 else yb

        def plane(zz):
            pick = jnp.concatenate([picks(zz * RING + i, at, size) for i in range(RING)], axis=0)
            place_ = rows(base + zz * (RING * size), RING * size)
            for lo in range(start, start + width, wide):
                lane = pl.ds(lo, min(wide, start + width - lo))
                made = jnp.dot(pick, source[:, lane], preferred_element_type=f32)
                if n == 5:
                    made = made + jnp.concatenate([exty[:, lane]] * RING, axis=0)
                ob[place_, lane] = made.astype(bf16)
            if n == 0:
                for i in range(RING):
                    tail = rows(zz * (RING * size) + i * size + 64, 16)
                    first = pl.ds(0, 2 * LANES)
                    ob[tail, first] = (ob[tail, first].astype(f32) + gate_rows(zz * RING + i)).astype(bf16)

        def go(k):
            dz = (k + 1) % RING
            plane((z + dz) % RING)

            @pl.when(dz > 0)
            def _():
                for dy in range(1, RING):
                    i = (dz - 1) * 3 + dy - 1
                    a_first(n, i).start()
                    b_first(n, i).start()
                straight(n, dz - 1).start()

            @pl.when(dz == 0)
            def _():
                for dy in range(1, RING):
                    straight(n, 2 + dy).start()
                keep(n).start()

        loop(RING, go)

    def forward(n):
        def go(i):
            a_first(n, i).wait_recv()
            a_second(n, i).start()
            b_first(n, i).wait_recv()
            b_second(n, i).start()

        loop(9, go)

    def built_sent(n):
        def go(i):
            a_first(n, i).wait_send()
            b_first(n, i).wait_send()

        loop(9, go)
        loop(6, lambda i: straight(n, i).wait_send())
        if n < 3:
            keep(n).wait()

    def forwards_sent(n):
        def go(i):
            a_second(n, i).wait_send()
            b_second(n, i).wait_send()

        loop(9, go)

    def arrived(n):
        def go(i):
            a_second(n, i).wait_recv()
            b_second(n, i).wait_recv()

        loop(9, go)
        loop(6, lambda i: straight(n, i).wait_recv())
        if n >= 3:
            keep(n).wait()

    span = 256

    def pair_x(j):
        at = rows(j * span, span)
        return remote(pas.at[at], pap.at[at], ps.at[j], pr.at[j], partner)

    def pair_y(j):
        at = rows(j * span, span)
        return remote(ras.at[at], rap.at[at], qs.at[j], qr.at[j], partner)

    def use_x(j):
        at = rows(j * span, span)
        part = jnp.dot(xin[at, :], wu[...], preferred_element_type=f32)
        pa[at, :] = part
        pas[at, :] = part.astype(bf16)
        pair_x(j).start()

    def use_y(j):
        at = rows(j * span, span)
        part = lax.dot_general(yin[at, :], wd[pl.ds(0, hid), :], NT, preferred_element_type=f32)
        ra[at, :] = part
        ras[at, :] = part.astype(bf16)
        pair_y(j).start()

    def meet(p):
        size, at = PARTS[p], PART_AT[p]
        shape = (size, 2 * LANES)
        lane = lax.broadcasted_iota(jnp.int32, shape, 1)
        row = at + lax.broadcasted_iota(jnp.int32, shape, 0)
        row_lane = jnp.where(row < RING * cap, 12 + row // cap, -1)
        square = at + lax.broadcasted_iota(jnp.int32, (size, LANES), 0) == lax.broadcasted_iota(
            jnp.int32, (size, LANES), 1
        )
        first = lax.broadcasted_iota(jnp.int32, (16, size), 0)
        which = (at + lax.broadcasted_iota(jnp.int32, (16, size), 1)) // cap
        gather = jnp.where(first == which, 1.0, 0.0).astype(bf16)

        def go(cc):
            xr_ = rows(cc * rb + at, size)
            yr_ = rows(at * COLUMNS + cc * size, size)
            tail = xin[rows(cc * rb + 64, 16), pl.ds(0, 2 * LANES)].astype(f32)
            p_ = pa[xr_, :] + pap[xr_, :].astype(f32)
            r = ra[yr_, :] + rap[yr_, :].astype(f32)
            gate = jnp.sum(tail[12:15, :LANES], axis=0, keepdims=True)
            gate = jnp.sum(jnp.where(square, gate, 0.0), axis=1, keepdims=True)
            logistic = jax.nn.sigmoid(p_)
            gated = gate * (p_ * logistic)
            ra[yr_, :] = gated
            pa[xr_, :] = gate * r * (logistic * (1.0 + p_ * (1.0 - logistic)))
            margin = jnp.sum(gated * r, axis=1, keepdims=True)
            hot = jnp.where(lane - cc * 16 == row_lane, 1.0, 0.0)
            acc[1:2, :] += 0.5 * jnp.sum(hot * margin, axis=0, keepdims=True)
            spot = rows(cc * 16, 16)
            summed = jnp.dot(gather, gated.astype(bf16), preferred_element_type=f32)
            if p == 0:
                acc[3:4, :] += tail[15:16]
                hst[spot, :] = summed
            else:
                hst[spot, :] += summed
            if p == 2:
                prs[spot, :] = r

        loop(COLUMNS, go)

    def side_rows():
        exty[...] = jnp.zeros_like(exty)
        tall = lax.broadcasted_iota(jnp.int32, (LANES, LANES), 0)
        for j in range(hw // LANES):
            lane = pl.ds(j * LANES, LANES)
            for b in range(RING):
                exty[12 + b : 13 + b, lane] = mb[b, 32 + j : 33 + j, :]
            terms = split3(mb[x, 52 + j : 53 + j, :]) + split3(mb[x + 1 - 2 * x_lo, 52 + j : 53 + j, :])
            block = jnp.zeros((LANES, LANES), f32)
            for i, term in enumerate(terms):
                block = jnp.where(tall == i, term, block)
            wd[pl.ds(hid, LANES), lane] = block.astype(bf16)

    wait_ring(1)
    start_ring(2)
    build(0)
    wait_ring(2)
    start_ring(3)
    build(1)
    forward(0)
    wait_ring(3)
    start_ring(4)
    build(2)
    forward(1)
    built_sent(0)
    built_sent(1)
    forward(2)
    built_sent(2)
    wait_ring(4)
    build(3)
    build(4)
    for copy in locals_[6:]:
        copy.wait()
    side_rows()
    for n in range(3):
        arrived(n)
    loop(2, use_x)
    forward(3)
    loop(5, use_x, 2)
    build(5)
    forward(4)
    arrived(3)
    loop(2, use_y)
    forward(5)
    arrived(4)
    loop(4, use_y, 2)
    loop(5, lambda j: pair_x(j).wait_recv())
    loop(2, lambda j: pair_y(j).wait_recv())
    meet(0)
    arrived(5)
    last_at = rows(4 * span, span)
    last_part = lax.dot_general(yin[last_at, :], wd[...], NT, preferred_element_type=f32)
    ra[last_at, :] = last_part[:, :hid]
    ras[last_at, :] = last_part[:, :hid].astype(bf16)
    pair_y(4).start()
    wst[...] = last_part[:, hid:]
    loop(4, lambda j: pair_y(j).wait_recv(), 2)
    meet(1)
    for n in range(3, 6):
        built_sent(n)
    for n in range(6):
        forwards_sent(n)
    loop(5, lambda j: pair_x(j).wait_send())
    for ring in rings:
        for copy in ring:
            copy.wait_send()
    pair_y(4).wait_recv()
    meet(2)
    loop(5, lambda j: pair_y(j).wait_send())

    wide_t = wst[...].T
    base_own = wide_t[0:1] + wide_t[1:2] + wide_t[2:3]
    base_other = wide_t[3:4] + wide_t[4:5] + wide_t[5:6]
    pairs = acc[3:4, :]
    terms = 0.5 * lax.dot_general(
        hst[...], prs[...], NT, precision=lax.Precision.HIGHEST, preferred_element_type=f32
    )
    named = lax.broadcasted_iota(jnp.int32, terms.shape, 0)
    terms += jnp.where(named == col * 16 + x, base_own, 0.0)
    terms += jnp.where(named == col * 16 + x + 1 - 2 * x_lo, base_other, 0.0)
    used = lax.broadcasted_iota(jnp.int32, (1, 2 * LANES), 1) % 16 >= 12
    chosen = jnp.where((named.astype(f32) == pairs) & used, terms, 0.0)
    acc[0:1, :] += jnp.sum(chosen, axis=0, keepdims=True)

    def along(d):
        return remote(acc, arb.at[d - 1], ar_s.at[d - 1], ar_r.at[d - 1], dev_x((x + d) % RING))

    def across(d):
        return remote(acc, arb.at[3 + d], ar_s.at[3 + d], ar_r.at[3 + d], dev_across((x + d) % RING))

    def around(k):
        return remote(acc, arc.at[k - 1], ar_s.at[6 + k], ar_r.at[6 + k], dev_col(plus(k // RING, k % RING)))

    ringed = [along(d) for d in (1, 3, 2)] + [across(d) for d in (0, 1, 3, 2)]
    for copy in ringed:
        copy.start()
    for copy in ringed:
        copy.wait()
    acc[...] = acc[...] + arb[0] + arb[1] + arb[2]
    acc[4:5, :] = arb[3, 0:1] + arb[4, 0:1] + arb[5, 0:1] + arb[6, 0:1]
    loop(COLUMNS, lambda k: around(k).start(), 1)
    loop(COLUMNS, lambda k: around(k).wait(), 1)
    total = acc[...]
    for k in range(COLUMNS - 1):
        total = total + arc[k]
    kl_row, kl_other = total[0:1], total[4:5]
    count = RING * COLUMNS * 2
    anchor = jnp.sum(kl_row + kl_other, axis=1, keepdims=True) / count
    signed = total[2:3]
    kept = jax.nn.sigmoid(kto_beta * signed * (total[1:2] - anchor))
    slope = -kto_beta * signed * kept * (1.0 - kept)
    small_out[...] = jnp.zeros_like(small_out)
    small_out[0:1, :] = 1.0 - kept
    small_out[1:2, :] = kl_row

    def scaled(source, dst, start, size, at):
        lane = lax.broadcasted_iota(jnp.int32, (size, 2 * LANES), 1)
        row = at + lax.broadcasted_iota(jnp.int32, (size, 2 * LANES), 0)
        row_lane = jnp.where(row < RING * cap, 12 + row // cap, -1)

        def go(cc):
            here = rows(start + cc * size, size)
            factor = jnp.sum(jnp.where(lane - cc * 16 == row_lane, slope, 0.0), axis=1, keepdims=True)
            dst[here, :] = (source[here, :] * factor).astype(bf16)

        loop(COLUMNS, go)

    quarter = hw // 2
    step = 640
    other = (1 - core) * quarter
    this = core * quarter
    hid_t = m2y.at[pl.ds(0, hid)]
    up_got, down_got = rap, m1y.at[pl.ds(0, hid)]
    up_out, down_out = pl.ds(0, hid), m1x.at[pl.ds(0, hid)]
    down_sent = pl.ds(quarter, quarter)

    def up_block(start, j):
        at = pl.ds(pl.multiple_of(start + j * step, LANES), step)
        return lax.dot_general(xin[:, at], pas[...], TN, preferred_element_type=f32)

    def down_block(start, j):
        at = pl.ds(pl.multiple_of(start + j * step, LANES), step)
        return jnp.dot(hid_t[...], yin[:, at], preferred_element_type=f32)

    def piece(j, base=0):
        return pl.ds(pl.multiple_of(base + j * step, LANES), step)

    def other_up(j):
        pap[piece(j), :] = up_block(other, j).astype(bf16)

    def other_down(j):
        ob[pl.ds(0, hid), piece(j, quarter)] = down_block(other, j).astype(bf16)

    def this_up(j):
        ob[piece(j), up_out] = (up_block(this, j) + up_got[piece(j), :].astype(f32)).astype(bf16)

    def this_down(j):
        down_out[:, piece(j)] = (down_block(this, j) + down_got[:, piece(j)].astype(f32)).astype(bf16)

    up_copy = remote(pap, up_got, g_s.at[0], g_r.at[0], sibling)
    down_copy = remote(ob.at[pl.ds(0, hid), down_sent], down_got, g_s.at[1], g_r.at[1], sibling)
    blocks = quarter // step
    scaled(pa, pas, 0, rb, 0)
    loop(blocks, other_up)
    up_copy.start()
    for p in range(3):
        scaled(ra, ras, PART_AT[p] * COLUMNS, PARTS[p], PART_AT[p])
    for j in range(slots // span):
        at = pl.ds(j * span, span)
        hid_t[:, at] = ras[at, :].T
    loop(blocks, other_down)
    down_copy.start()
    up_copy.wait_recv()
    loop(blocks, this_up)
    up_done = pltpu.make_async_copy(ob.at[pl.ds(0, quarter), up_out], up_hbm, lsem.at[0])
    up_done.start()
    down_copy.wait_recv()
    loop(blocks, this_down)
    down_done = pltpu.make_async_copy(down_out, down_hbm, lsem.at[1])
    down_done.start()
    up_copy.wait_send()
    down_copy.wait_send()
    up_done.wait()
    down_done.wait()


def local(
    tokens, router, expert_ids, w_up, w_down, readout, ref_logp, labels, prompt_read, kl_pair, kl_ref
):
    experts = lax.axis_size("expert")
    tr, width = tokens.shape
    top = expert_ids.shape[1]
    cap = 4 * tr * top // (5 * experts)
    hid = w_up.shape[2]
    hw = width // 2
    x_lo, core, x_hi, col = place()
    x = x_hi * 2 + x_lo

    slots = COLUMNS * META
    quarter = hw // 2
    dma = pltpu.SemaphoreType.DMA
    any_ = pl.BlockSpec(memory_space=pl.ANY)
    vmem = pl.BlockSpec(memory_space=pltpu.VMEM)
    smem = pl.BlockSpec(memory_space=pltpu.SMEM)
    up, down, small = pl.pallas_call(
        functools.partial(kernel, cap, hw),
        out_shape=(
            jax.ShapeDtypeStruct((quarter, hid), bf16),
            jax.ShapeDtypeStruct((hid, quarter), bf16),
            jax.ShapeDtypeStruct((8, 2 * LANES), f32),
        ),
        in_specs=[any_, any_, any_, vmem, vmem, vmem, smem, smem, smem, any_, any_],
        out_specs=(any_, any_, vmem),
        scratch_shapes=[
            pltpu.VMEM((RING * tr, hw), bf16),
            pltpu.VMEM((RING * tr, hw), bf16),
            pltpu.VMEM((RING, META, LANES), f32),
            pltpu.VMEM((slots, hw), bf16),
            pltpu.VMEM((slots, hw), bf16),
            pltpu.VMEM((slots, hw), bf16),
            pltpu.VMEM((max(9 * META, hid), quarter), bf16),
            pltpu.VMEM((9 * META, quarter), bf16),
            pltpu.VMEM((max(9 * META, hid), quarter), bf16),
            pltpu.VMEM((max(9 * META, hid), quarter), bf16),
            pltpu.VMEM((hw, hid), bf16),
            pltpu.VMEM((hid + LANES, hw), bf16),
            pltpu.VMEM((slots, hid), f32),
            pltpu.VMEM((slots, hid), f32),
            pltpu.VMEM((slots, hid), bf16),
            pltpu.VMEM((slots, hid), bf16),
            pltpu.VMEM((slots, hid), bf16),
            pltpu.VMEM((slots, hid), bf16),
            pltpu.VMEM((COLUMNS * 16, hid), f32),
            pltpu.VMEM((COLUMNS * 16, hid), f32),
            pltpu.VMEM((COLUMNS * 16, LANES), f32),
            pltpu.VMEM((16, hw), f32),
            pltpu.VMEM((RING, META, LANES), f32),
            pltpu.VMEM((2 * COLUMNS, tr), f32),
            pltpu.VMEM((8, 2 * LANES), f32),
            pltpu.VMEM((2 * RING - 1, 8, 2 * LANES), f32),
            pltpu.VMEM((COLUMNS - 1, 8, 2 * LANES), f32),
            dma((8,)), dma((6,)),
            dma((15,)), dma((15,)),
        ]
        + [dma((6, 9)) for _ in range(8)]
        + [dma((6, 6)) for _ in range(2)]
        + [
            dma((5,)), dma((5,)),
            dma((5,)), dma((5,)),
            dma((22,)), dma((22,)),
            dma((2,)), dma((2,)),
        ],
        compiler_params=pltpu.CompilerParams(
            collective_id=0, has_side_effects=True, vmem_limit_bytes=63 * 2**20
        ),
        cost_estimate=pl.CostEstimate(flops=40 * 10**9, bytes_accessed=30 * 10**6, transcendentals=10**6),
        name="routed_step",
    )(
        tokens, readout, router.T, expert_ids.T, ref_logp.reshape(1, tr), prompt_read, labels, kl_pair, kl_ref,
        w_up[0], w_down[0],
    )
    here = col * 16 + 12 + x
    losses = lax.dynamic_slice(small, (0, here), (1, 1)).reshape(1)
    kl_terms = lax.dynamic_slice(small, (1, here), (1, 1)).reshape(1)
    return (up * bf16(loss_scale))[None], (down * bf16(loss_scale))[None], losses, kl_terms


def solution(mesh):
    return jax.shard_map(
        local,
        mesh=mesh,
        in_specs=(
            P(("dp", "expert"), None),
            P(),
            P(("dp", "expert"), None),
            P("expert", None, None),
            P("expert", None, None),
            P(("dp", "expert"), None),
            P(("dp", "expert")),
            P(("dp", "expert")),
            P(("dp", "expert"), None),
            P(("dp", "expert")),
            P(("dp", "expert")),
        ),
        out_specs=(
            P("expert", "dp", None),
            P("expert", None, "dp"),
            P(("dp", "expert")),
            P(("dp", "expert")),
        ),
        check_vma=False,
    )
```
